128 devices in a mesh: blk: 16 (over x, y), grp: 8 (over z, core).
Axes of the slice: x: 4, y: 4, z: 4, core: 2. Of those that a mesh axis runs over, the one named last changes fastest.
Arguments:
- nodes: bfloat16 [131072, 128], P(('blk', 'grp')), may hold values from -6 to 6
- edges: bfloat16 [524288, 128], P(('blk', 'grp')), may hold values from -6 to 6
- wanted_rows: int32 [2048, 128], P(('blk', 'grp')), may hold values from 0 to 1023, as said below
- sender_slot: int32 [524288], P(('blk', 'grp')), may hold values from 0 to 2047, as said below
- receiver: int32 [524288], P(('blk', 'grp')), may hold values from 0 to 1023
- w_edge_in: bfloat16 [384, 512], replicated, may hold values from -0.3125 to 0.3125
- w_edge_out: bfloat16 [512, 128], replicated, may hold values from -0.25 to 0.25
- w_node_in: bfloat16 [256, 512], replicated, may hold values from -0.375 to 0.375
- w_node_out: bfloat16 [512, 128], replicated, may hold values from -0.25 to 0.25
- node_cot: bfloat16 [131072, 128], P(('blk', 'grp')), may hold values from -6 to 6
- edge_cot: bfloat16 [524288, 128], P(('blk', 'grp')), may hold values from -6 to 6
Outputs:
- new_nodes: bfloat16 [131072, 128], P(('blk', 'grp'))
- new_edges: bfloat16 [524288, 128], P(('blk', 'grp'))
- node_grad: float32 [131072, 128], P(('blk', 'grp'))
- edge_grad: float32 [524288, 128], P(('blk', 'grp'))
- grad_edge_in: float32 [384, 512], replicated
- grad_edge_out: float32 [512, 128], replicated
- grad_node_in: float32 [256, 512], replicated
- grad_node_out: float32 [512, 128], replicated
The draws below stay inside these ranges and needn't reach their ends.
Inputs may be any that keep to these rules, and one draw needn't show every extreme that they name: `wanted_rows`: row 16 d + p holds 128 distinct local grain rows of the device at blk index p and at device d's grp index. `sender_slot`: on each device, every one of its 2048 slots is named by one or more contacts.
All inputs are finite; a program needn't handle non-finite values.
Results may differ from the reference program's by a relative error of at most 0.015.
Values may be sent and summed in bfloat16 or wider, within the bound.
A program may use at most 128 MiB of HBM per device.

```python
import jax
import jax.numpy as jnp
from jax import lax

L = 128
H = 512
G_DEV = 1024
E_DEV = 4096
CAP = 128
GRAINS = 131072
CONTACTS = 524288
N_BLK = 16
N_GRP = 8
DEVICES = 128


def draw_wanted_rows(key, part):
    key = jax.random.fold_in(key, 11)
    subkeys = jax.random.split(key, N_BLK * DEVICES)

    def one_row(subkey):
        return jax.random.permutation(subkey, G_DEV)[:CAP]
    return jax.vmap(one_row)(subkeys).astype(jnp.int32)


def draw_sender_slot(key, part):
    key = jax.random.fold_in(key, 23)
    slot_count = N_BLK * CAP
    first_key, second_key = jax.random.split(key)
    extra = jax.random.randint(first_key, (DEVICES, E_DEV - slot_count), 0, slot_count, dtype=jnp.int32)
    base = jnp.broadcast_to(jnp.arange(slot_count, dtype=jnp.int32)[None, :], (DEVICES, slot_count))
    joined = jnp.concatenate([base, extra], axis=1)
    subkeys = jax.random.split(second_key, DEVICES)

    def shuffle(subkey, row_values):
        return jax.random.permutation(subkey, row_values)
    return jax.vmap(shuffle)(subkeys, joined).reshape(-1).astype(jnp.int32)


def touch_ends(values, key, smallest, largest):
    longest = values.shape.index(max(values.shape))
    spots = []
    for shift in (0, 1):
        where = [jax.random.randint(jax.random.fold_in(key, axis), (), 0, length) for axis, length in enumerate(values.shape)]
        where[longest] = (where[longest] + shift) % values.shape[longest]
        spots.append(tuple(where))
    return values.at[spots[0]].set(smallest).at[spots[1]].set(largest)


def block_scale(stream_key, dims, cuts, low, top_value):
    level = 1.0
    for position, parts in cuts:
        heights = jax.random.uniform(jax.random.fold_in(jax.random.fold_in(stream_key, 6), position), (parts,), jnp.float32, low / len(cuts), top_value / len(cuts))
        level = level * jnp.repeat(jnp.exp(heights), dims[position] // parts).reshape((-1,) + (1,) * (len(dims) - 1 - position))
    return level


def bell_draw(stream_key, extent, width, bound, cuts=(), held_as=jnp.bfloat16):
    values = width * jax.random.normal(stream_key, extent, jnp.float32)
    if cuts:
        values = values * block_scale(stream_key, extent, cuts, -0.22, 0.18)
    return jnp.clip(values, -bound, bound).astype(held_as)


def setup_inputs(seed: int = 0) -> dict:
    streams_of = jax.random.split(jax.random.key(seed), 12)
    return {
        "nodes": bell_draw(streams_of[0], (GRAINS, L), 1.0, 6.0, ((0, 128),)),
        "edges": bell_draw(streams_of[1], (CONTACTS, L), 1.0, 6.0, ((0, 128),)),
        "wanted_rows": draw_wanted_rows(jax.random.fold_in(streams_of[11], 71), 0),
        "sender_slot": draw_sender_slot(jax.random.fold_in(streams_of[11], 71), 0),
        "receiver": touch_ends(jax.random.randint(streams_of[4], (CONTACTS,), 0, G_DEV), jax.random.fold_in(streams_of[4], 1), 0, G_DEV - 1).astype(jnp.int32),
        "w_edge_in": bell_draw(streams_of[5], (3 * L, H), (3 * L) ** -0.5, 0.3125),
        "w_edge_out": bell_draw(streams_of[6], (H, L), H ** -0.5, 0.25),
        "w_node_in": bell_draw(streams_of[7], (2 * L, H), (2 * L) ** -0.5, 0.375),
        "w_node_out": bell_draw(streams_of[8], (H, L), H ** -0.5, 0.25),
        "node_cot": bell_draw(streams_of[9], (GRAINS, L), 1.0, 6.0, ((0, 128),)),
        "edge_cot": bell_draw(streams_of[10], (CONTACTS, L), 1.0, 6.0, ((0, 128),)),
    }


EPSILON = 1e-05

def contract_rows(left, right):
    return lax.dot_general(left, right, (((0,), (0,)), ((), ())), preferred_element_type=jnp.float32)

def contract_cols(left, right):
    return lax.dot_general(left, right, (((1,), (1,)), ((), ())), preferred_element_type=jnp.float32)

def silu_grad(value):
    sigm = jax.nn.sigmoid(value)
    return sigm * (1.0 + value * (1.0 - sigm))

def layer_norm(value):
    center = value - lax.optimization_barrier(jnp.mean(value, axis=-1, keepdims=True))
    sigma = jnp.sqrt(lax.optimization_barrier(jnp.mean(center * center, axis=-1, keepdims=True)) + EPSILON)
    return (center / sigma, sigma)

def norm_back(upstream, normed, sigma):
    first = lax.optimization_barrier(jnp.mean(upstream, axis=-1, keepdims=True))
    second = lax.optimization_barrier(jnp.mean(upstream * normed, axis=-1, keepdims=True))
    return (upstream - first - normed * second) / sigma

def mlp_forward(stacked, w_first, w_second):
    pre_act = jnp.dot(stacked, w_first, preferred_element_type=jnp.float32)
    hidden = jax.nn.silu(pre_act).astype(jnp.bfloat16)
    out_act = jnp.dot(hidden, w_second, preferred_element_type=jnp.float32)
    normed, sigma = layer_norm(out_act)
    return (pre_act, hidden, normed, sigma)

def mlp_backward(stacked, pre_act, hidden, normed, sigma, upstream, w_first, w_second):
    d_out = norm_back(upstream, normed, sigma).astype(jnp.bfloat16)
    grad_second = contract_rows(hidden, d_out)
    d_pre = (contract_cols(d_out, w_second) * silu_grad(pre_act)).astype(jnp.bfloat16)
    grad_first = contract_rows(stacked, d_pre)
    d_input = contract_cols(d_pre, w_first)
    return (d_input, grad_first, grad_second)

def reference(nodes, edges, wanted_rows, sender_slot, receiver, w_edge_in, w_edge_out, w_node_in, w_node_out, node_cot, edge_cot):
    latent = nodes.shape[1]
    grains = nodes.shape[0]
    contacts = edges.shape[0]
    dev_of = jnp.arange(contacts, dtype=jnp.int32) // E_DEV
    grp_of = dev_of % N_GRP
    peer = sender_slot // CAP
    column = sender_slot % CAP
    local_row = wanted_rows[(dev_of * N_BLK + peer).astype(jnp.int32), column]
    sender_ids = ((peer * N_GRP + grp_of) * G_DEV + local_row).astype(jnp.int32)
    receiver_ids = (dev_of * G_DEV + receiver).astype(jnp.int32)
    blocks = edges.shape[0] // E_DEV
    edge_blocks = edges.reshape(blocks, E_DEV, latent)
    send_blocks = sender_ids.reshape(blocks, E_DEV)
    recv_blocks = receiver_ids.reshape(blocks, E_DEV)
    cot_blocks = edge_cot.reshape(blocks, E_DEV, latent)

    def edge_stack(block_edges, senders, receivers):
        return jnp.concatenate([block_edges, nodes[senders], nodes[receivers]], axis=1)

    def forward_block(items):
        block_edges, senders, receivers = items
        stacked = edge_stack(block_edges, senders, receivers)
        pre_act, hidden, normed, sigma = mlp_forward(stacked, w_edge_in, w_edge_out)
        message = normed.astype(jnp.bfloat16)
        updated = (block_edges.astype(jnp.float32) + message.astype(jnp.float32)).astype(jnp.bfloat16)
        return (message, updated)
    messages, new_edges = lax.map(forward_block, (edge_blocks, send_blocks, recv_blocks))
    messages = messages.reshape(contacts, latent)
    new_edges = new_edges.reshape(contacts, latent)
    inbound = jax.ops.segment_sum(messages.astype(jnp.float32), receiver_ids, num_segments=grains).astype(jnp.bfloat16)
    node_input = jnp.concatenate([nodes, inbound], axis=1)
    node_pre, node_hidden, node_norm, node_sigma = mlp_forward(node_input, w_node_in, w_node_out)
    new_nodes = (nodes.astype(jnp.float32) + node_norm).astype(jnp.bfloat16)
    d_node_input, g_node_in, g_node_out = mlp_backward(node_input, node_pre, node_hidden, node_norm, node_sigma, node_cot.astype(jnp.float32), w_node_in, w_node_out)
    d_inbound = d_node_input[:, latent:]

    def backward_block(carry, items):
        acc_nodes, acc_in, acc_out = carry
        block_edges, senders, receivers, block_cot = items
        stacked = edge_stack(block_edges, senders, receivers)
        pre_act, hidden, normed, sigma = mlp_forward(stacked, w_edge_in, w_edge_out)
        upstream = block_cot.astype(jnp.float32) + d_inbound[receivers]
        d_input, g_first, g_second = mlp_backward(stacked, pre_act, hidden, normed, sigma, upstream, w_edge_in, w_edge_out)
        acc_nodes = acc_nodes.at[senders].add(d_input[:, latent:2 * latent])
        acc_nodes = acc_nodes.at[receivers].add(d_input[:, 2 * latent:])
        block_grad = block_cot.astype(jnp.float32) + d_input[:, :latent]
        return ((acc_nodes, acc_in + g_first, acc_out + g_second), block_grad)
    start = (jnp.zeros((grains, latent), jnp.float32), jnp.zeros(w_edge_in.shape, jnp.float32), jnp.zeros(w_edge_out.shape, jnp.float32))
    (acc_nodes, g_edge_in, g_edge_out), edge_grad = lax.scan(backward_block, start, (edge_blocks, send_blocks, recv_blocks, cot_blocks))
    edge_grad = edge_grad.reshape(contacts, latent)
    node_grad = node_cot.astype(jnp.float32) + d_node_input[:, :latent] + acc_nodes
    edge_scale = 1.0 / jnp.sqrt(jnp.float32(contacts))
    node_scale = 1.0 / jnp.sqrt(jnp.float32(grains))
    return (new_nodes, new_edges, node_grad, edge_grad, g_edge_in * edge_scale, g_edge_out * edge_scale, g_node_in * node_scale, g_node_out * node_scale)
```

```python
import functools

import jax
import jax.numpy as jnp
from jax import lax
from jax.experimental import pallas as pl
from jax.experimental.pallas import tpu as pltpu
from jax.sharding import PartitionSpec as P

EPSILON = 1e-05
L = 128
H = 512
NB = 16
NG = 8
GR = 1024
E = 4096
T = 512
NT = E // T
F32 = jnp.float32
BF16 = jnp.bfloat16
I16 = jnp.int16
VMEM_LIMIT = 60 * 1024 * 1024
MESH = pl.DeviceIdType.MESH


def mm(a, b):
    return jnp.dot(a, b, preferred_element_type=F32)


def mm_nt(a, b):
    return lax.dot_general(a, b, (((1,), (1,)), ((), ())), preferred_element_type=F32)


def mm_tn(a, b):
    return lax.dot_general(a, b, (((0,), (0,)), ((), ())), preferred_element_type=F32)


def column(rows):
    parts = [
        jnp.transpose(jnp.broadcast_to(rows[i : i + 1, :], (128, 128)))
        for i in range(rows.shape[0])
    ]
    return parts[0] if len(parts) == 1 else jnp.concatenate(parts, axis=0)


def pick(col, width):
    col = col.astype(I16)
    lane = lax.broadcasted_iota(jnp.int32, col.shape, 1).astype(I16)
    one = jnp.ones(col.shape, BF16)
    zero = jnp.zeros(col.shape, BF16)
    return jnp.concatenate(
        [jnp.where(col == lane + I16(128 * j), one, zero) for j in range(width // 128)], axis=1
    )


def spread(rows, width):
    outs = []
    for i in range(rows.shape[0]):
        ids = jnp.broadcast_to(rows[i : i + 1, :], (128, 128)).astype(I16)
        sub = lax.broadcasted_iota(jnp.int32, (128, 128), 0).astype(I16)
        one = jnp.ones((128, 128), BF16)
        zero = jnp.zeros((128, 128), BF16)
        outs.append(
            jnp.concatenate(
                [jnp.where(ids == sub + I16(128 * j), one, zero) for j in range(width // 128)],
                axis=0,
            )
        )
    return outs[0] if len(outs) == 1 else jnp.concatenate(outs, axis=1)


def halves(value, high):
    zero = jnp.zeros_like(value)
    return jnp.concatenate(
        [jnp.where(high, zero, value), jnp.where(high, value, zero)], axis=1
    ).astype(BF16)


def layer_norm(value):
    center = value - jnp.mean(value, axis=-1, keepdims=True)
    inv = lax.rsqrt(jnp.mean(center * center, axis=-1, keepdims=True) + EPSILON)
    return center * inv, inv


def norm_back(upstream, normed, inv):
    first = jnp.mean(upstream, axis=-1, keepdims=True)
    second = jnp.mean(upstream * normed, axis=-1, keepdims=True)
    return (upstream - first - normed * second) * inv


def silu_pair(pre):
    sig = 0.5 * jnp.tanh(0.5 * pre) + 0.5
    hid = pre * sig
    return hid.astype(BF16), sig + hid * (1.0 - sig)


def greet(peers):
    barrier = pltpu.get_barrier_semaphore()
    for peer in peers:
        pl.semaphore_signal(barrier, inc=1, device_id=peer, device_id_type=MESH)
    pl.semaphore_wait(barrier, len(peers))


def fetch_kernel(wanted, nodes, rows, asked, staged, s1, r1, s2, r2, local):
    me = lax.axis_index("blk")
    grp = lax.axis_index("grp")
    greet([(lax.rem(me + k, NB), grp) for k in range(1, NB)])

    def ask(k):
        return pltpu.make_async_remote_copy(
            src_ref=wanted.at[lax.rem(me + k, NB)],
            dst_ref=asked.at[me],
            send_sem=s1.at[k],
            recv_sem=r1.at[k],
            device_id=(lax.rem(me + k, NB), grp),
            device_id_type=MESH,
        )

    def give(k):
        return pltpu.make_async_remote_copy(
            src_ref=staged.at[k],
            dst_ref=rows.at[me],
            send_sem=s2.at[k],
            recv_sem=r2.at[k],
            device_id=(lax.rem(me + NB - k, NB), grp),
            device_id_type=MESH,
        )

    for k in range(1, NB):
        ask(k).start()
    own = pltpu.make_async_copy(wanted.at[me], asked.at[me], local)
    own.start()
    own.wait()
    rows[me] = mm(pick(column(asked[me]), GR), nodes[...]).astype(BF16)

    def answer(k, carry):
        ask(k).wait_recv()
        src = lax.rem(me + NB - k, NB)
        staged[k] = mm(pick(column(asked[src]), GR), nodes[...]).astype(BF16)
        give(k).start()
        return carry

    lax.fori_loop(1, NB, answer, 0)
    for k in range(1, NB):
        ask(k).wait_send()
        give(k).wait()


def whole(n):
    return [pl.BlockSpec(memory_space=pltpu.VMEM)] * n


def fetch(wanted, nodes):
    return pl.pallas_call(
        fetch_kernel,
        name="fetch_rows",
        out_shape=(
            jax.ShapeDtypeStruct((NB, 128, L), BF16),
            jax.ShapeDtypeStruct((NB, 1, 128), jnp.int32),
        ),
        in_specs=whole(2),
        out_specs=whole(2),
        scratch_shapes=[
            pltpu.VMEM((NB, 128, L), BF16),
            pltpu.SemaphoreType.DMA((NB,)),
            pltpu.SemaphoreType.DMA((NB,)),
            pltpu.SemaphoreType.DMA((NB,)),
            pltpu.SemaphoreType.DMA((NB,)),
            pltpu.SemaphoreType.DMA,
        ],
        compiler_params=pltpu.CompilerParams(
            collective_id=0, has_side_effects=True, vmem_limit_bytes=VMEM_LIMIT
        ),
    )(wanted, nodes)


def store_block(total, block, value):
    value = value.astype(BF16)
    for half in range(2):
        for i in range(4):
            for j in range(4):
                total[half, 4 * i + j, 16 * block : 16 * block + 16, :] = value[
                    64 * half + 16 * i : 64 * half + 16 * i + 16, 128 * j : 128 * j + 128
                ]


def net_kernel(
    nodes,
    edges,
    slot_rows,
    slot,
    receiver,
    w_ein,
    w_eout,
    w_nin,
    w_nout,
    node_cot,
    edge_cot,
    new_nodes,
    new_edges,
    edge_grad,
    node_part,
    slot_grad,
    total,
    stacked,
    hidden,
    slope,
    normed,
    inverse,
    d_pre_all,
    d_out_all,
    slots2,
    nodes2,
    acc_node,
    acc_slot,
    pick_recv,
):
    tr = T // 128
    nodes2[:, :L] = nodes[: GR // 2, :]
    nodes2[:, L:] = nodes[GR // 2 :, :]
    for p in range(8):
        slots2[128 * p : 128 * p + 128, :L] = slot_rows[p]
        slots2[128 * p : 128 * p + 128, L:] = slot_rows[p + 8]
    acc_node[...] = jnp.zeros_like(acc_node)
    acc_slot[...] = jnp.zeros_like(acc_slot)

    def forward(t, carry):
        rows = pl.ds(pl.multiple_of(t * T, T), T)
        ids = pl.ds(t * tr, tr)
        recv = receiver[ids]
        recv = recv.reshape(tr, 128)
        send = slot[ids].reshape(tr, 128)
        recv_col = column(recv)
        send_col = column(send)
        recv_high = recv_col >= 512
        hot = pick(recv_col & 511, 512)
        pick_recv[rows, :] = hot
        both = mm(hot, nodes2[...])
        recv_rows = jnp.where(recv_high, both[:, L:], both[:, :L]).astype(BF16)
        both = mm(pick(send_col & 1023, 1024), slots2[...])
        send_rows = jnp.where(send_col >= 1024, both[:, L:], both[:, :L]).astype(BF16)
        edge = edges[rows, :]
        stacked[rows, :L] = edge
        stacked[rows, L : 2 * L] = send_rows
        stacked[rows, 2 * L :] = recv_rows
        pre = mm(stacked[rows, :], w_ein[...])
        hid, slp = silu_pair(pre)
        hidden[rows, :] = hid
        slope[rows, :] = slp.astype(BF16)
        norm, inv = layer_norm(mm(hid, w_eout[...]))
        normed[rows, :] = norm
        inverse[rows, :] = jnp.broadcast_to(inv, (T, L))
        message = norm.astype(BF16).astype(F32)
        new_edges[rows, :] = (edge.astype(F32) + message).astype(BF16)
        acc_node[...] += mm(spread(recv & 511, 512), halves(message, recv_high))
        return carry

    lax.fori_loop(0, NT, forward, 0)

    inbound = jnp.concatenate([acc_node[:, :L], acc_node[:, L:]], axis=0).astype(BF16)
    node = nodes[...]
    node_input = jnp.concatenate([node, inbound], axis=1)
    hid, slp = silu_pair(mm(node_input, w_nin[...]))
    norm, inv = layer_norm(mm(hid, w_nout[...]))
    new_nodes[...] = (node.astype(F32) + norm).astype(BF16)
    cot = node_cot[...].astype(F32)
    d_out = norm_back(cot, norm, inv).astype(BF16)
    store_block(total, 6, mm_tn(d_out, hid))
    d_pre = (mm_nt(d_out, w_nout[...]) * slp).astype(BF16)
    d_in = mm_nt(d_pre, w_nin[...])
    node_part[...] = cot + d_in[:, :L]
    d_inbound = d_in[:, L:].astype(BF16)
    nodes2[:, :L] = d_inbound[: GR // 2, :]
    nodes2[:, L:] = d_inbound[GR // 2 :, :]
    g_in = mm_tn(node_input, d_pre)
    store_block(total, 4, g_in[:128])
    store_block(total, 5, g_in[128:])
    acc_node[...] = jnp.zeros_like(acc_node)

    def backward(t, carry):
        rows = pl.ds(pl.multiple_of(t * T, T), T)
        ids = pl.ds(t * tr, tr)
        recv = receiver[ids].reshape(tr, 128)
        send = slot[ids].reshape(tr, 128)
        recv_high = column(recv) >= 512
        send_high = column(send) >= 1024
        both = mm(pick_recv[rows, :], nodes2[...])
        cot = edge_cot[rows, :].astype(F32)
        upstream = cot + jnp.where(recv_high, both[:, L:], both[:, :L])
        d_out = norm_back(upstream, normed[rows, :], inverse[rows, :]).astype(BF16)
        d_out_all[rows, :] = d_out
        d_pre = (mm_nt(d_out, w_eout[...]) * slope[rows, :].astype(F32)).astype(BF16)
        d_pre_all[rows, :] = d_pre
        d_in = mm_nt(d_pre, w_ein[...])
        edge_grad[rows, :] = cot + d_in[:, :L]
        acc_slot[...] += mm(spread(send & 1023, 1024), halves(d_in[:, L : 2 * L], send_high))
        acc_node[...] += mm(spread(recv & 511, 512), halves(d_in[:, 2 * L :], recv_high))
        return carry

    lax.fori_loop(0, NT, backward, 0)
    node_part[: GR // 2, :] += acc_node[:, :L]
    node_part[GR // 2 :, :] += acc_node[:, L:]
    for p in range(8):
        slot_grad[p] = acc_slot[128 * p : 128 * p + 128, :L].astype(BF16)
        slot_grad[p + 8] = acc_slot[128 * p : 128 * p + 128, L:].astype(BF16)
    store_block(total, 3, mm_tn(d_out_all[...], hidden[...]))
    for b in range(3):
        store_block(total, b, mm_tn(stacked[:, 128 * b : 128 * b + 128], d_pre_all[...]))


def net(*args):
    return pl.pallas_call(
        net_kernel,
        name="edge_and_node_nets",
        out_shape=(
            jax.ShapeDtypeStruct((GR, L), BF16),
            jax.ShapeDtypeStruct((E, L), BF16),
            jax.ShapeDtypeStruct((E, L), F32),
            jax.ShapeDtypeStruct((GR, L), F32),
            jax.ShapeDtypeStruct((NB, 128, L), BF16),
            jax.ShapeDtypeStruct((2, NB, 112, L), BF16),
        ),
        in_specs=whole(11),
        out_specs=whole(6),
        scratch_shapes=[
            pltpu.VMEM((E, 3 * L), BF16),
            pltpu.VMEM((E, H), BF16),
            pltpu.VMEM((E, H), BF16),
            pltpu.VMEM((E, L), F32),
            pltpu.VMEM((E, L), F32),
            pltpu.VMEM((E, H), BF16),
            pltpu.VMEM((E, L), BF16),
            pltpu.VMEM((GR, 2 * L), BF16),
            pltpu.VMEM((GR // 2, 2 * L), BF16),
            pltpu.VMEM((GR // 2, 2 * L), F32),
            pltpu.VMEM((GR, 2 * L), F32),
            pltpu.VMEM((E, 512), BF16),
        ],
        compiler_params=pltpu.CompilerParams(vmem_limit_bytes=VMEM_LIMIT),
    )(*args)


def share_kernel(
    slot_grad, total, slot_in, out, half_in, mine, piece_in, own, z_in, pair_s, pair_r, ss, sr,
    ps, pr, zs, zr, os, orr, last_s, last_r,
):
    me = lax.axis_index("blk")
    grp = lax.axis_index("grp")
    core = lax.rem(grp, 2)
    zpos = grp // 2
    other = grp + 1 - 2 * core
    line = [(lax.rem(me + k, NB), grp) for k in range(1, NB)]
    stack = [(me, lax.rem(grp + 2 * k, NG)) for k in range(1, 4)]
    greet(line + stack + [(me, other)])

    def remote(src, dst, send, recv, to):
        return pltpu.make_async_remote_copy(
            src_ref=src, dst_ref=dst, send_sem=send, recv_sem=recv, device_id=to,
            device_id_type=MESH,
        )

    pair = remote(total.at[1 - core], half_in, pair_s, pair_r, (me, other))
    pair.start()

    def give_slot(k):
        to = lax.rem(me + k, NB)
        return remote(slot_grad.at[to], slot_in.at[me], ss.at[k], sr.at[k], (to, grp))

    for k in range(1, NB):
        give_slot(k).start()
    slot_in[me] = slot_grad[me]
    pair.wait()
    mine[...] = (total[core].astype(F32) + half_in[...].astype(F32)).astype(BF16)

    def give_piece(k):
        to = lax.rem(me + k, NB)
        return remote(mine.at[to], piece_in.at[me], ps.at[k], pr.at[k], (to, grp))

    for k in range(1, NB):
        give_piece(k).start()
    piece_in[me] = mine[me]
    for k in range(1, NB):
        give_piece(k).wait()
    acc = piece_in[0].astype(F32)
    for q in range(1, NB):
        acc = acc + piece_in[q].astype(F32)
    own[...] = acc.astype(BF16)

    def give_z(k):
        return remote(own, z_in.at[zpos], zs.at[k], zr.at[k], stack[k - 1])

    for k in range(1, 4):
        give_z(k).start()
    z_in[zpos] = own[...]
    for k in range(1, 4):
        give_z(k).wait()
    acc = z_in[0].astype(F32)
    for q in range(1, 4):
        acc = acc + z_in[q].astype(F32)
    out[core, me] = acc.astype(BF16)

    def give_out(k):
        to = lax.rem(me + k, NB)
        return remote(out.at[core, me], out.at[core, me], os.at[k], orr.at[k], (to, grp))

    for k in range(1, NB):
        give_out(k).start()
    for k in range(1, NB):
        give_out(k).wait()
    last = remote(out.at[core], out.at[core], last_s, last_r, (me, other))
    last.start()
    for k in range(1, NB):
        give_slot(k).wait()
    last.wait()


def share(slot_grad, total):
    sem = pltpu.SemaphoreType.DMA
    return pl.pallas_call(
        share_kernel,
        name="share_grads",
        out_shape=(
            jax.ShapeDtypeStruct((NB, 128, L), BF16),
            jax.ShapeDtypeStruct((2, NB, 112, L), BF16),
        ),
        in_specs=whole(2),
        out_specs=whole(2),
        scratch_shapes=[
            pltpu.VMEM((NB, 112, L), BF16),
            pltpu.VMEM((NB, 112, L), BF16),
            pltpu.VMEM((NB, 112, L), BF16),
            pltpu.VMEM((112, L), BF16),
            pltpu.VMEM((4, 112, L), BF16),
            sem,
            sem,
            sem((NB,)),
            sem((NB,)),
            sem((NB,)),
            sem((NB,)),
            sem((4,)),
            sem((4,)),
            sem((NB,)),
            sem((NB,)),
            sem,
            sem,
        ],
        compiler_params=pltpu.CompilerParams(
            collective_id=1, has_side_effects=True, vmem_limit_bytes=VMEM_LIMIT
        ),
    )(slot_grad, total)


def finish_kernel(
    edge_scale, node_scale, slot_in, asked, node_part, out, node_grad, g_ein, g_eout, g_nin, g_nout
):
    acc = node_part[...]
    for q in range(0, NB, 4):
        ids = jnp.concatenate([asked[q + i] for i in range(4)], axis=0)
        vals = jnp.concatenate([slot_in[q + i] for i in range(4)], axis=0)
        acc = acc + mm(spread(ids, GR), vals)
    node_grad[...] = acc

    def block(b, scale):
        lines = []
        for half in range(2):
            for i in range(4):
                lines.append(
                    jnp.concatenate(
                        [out[half, 4 * i + j, 16 * b : 16 * b + 16, :] for j in range(4)], axis=1
                    )
                )
        return jnp.concatenate(lines, axis=0).astype(F32) * scale

    for b in range(3):
        g_ein[128 * b : 128 * b + 128, :] = block(b, edge_scale)
    for b in range(2):
        g_nin[128 * b : 128 * b + 128, :] = block(4 + b, node_scale)
    g_eout[...] = jnp.transpose(block(3, edge_scale))
    g_nout[...] = jnp.transpose(block(6, node_scale))


def finish(slot_in, asked, node_part, out):
    return pl.pallas_call(
        functools.partial(
            finish_kernel, float((E * NB * NG) ** -0.5), float((GR * NB * NG) ** -0.5)
        ),
        name="finish",
        out_shape=(
            jax.ShapeDtypeStruct((GR, L), F32),
            jax.ShapeDtypeStruct((3 * L, H), F32),
            jax.ShapeDtypeStruct((H, L), F32),
            jax.ShapeDtypeStruct((2 * L, H), F32),
            jax.ShapeDtypeStruct((H, L), F32),
        ),
        in_specs=whole(4),
        out_specs=whole(5),
        compiler_params=pltpu.CompilerParams(vmem_limit_bytes=VMEM_LIMIT),
    )(slot_in, asked, node_part, out)


def on_device(
    nodes,
    edges,
    wanted_rows,
    sender_slot,
    receiver,
    w_edge_in,
    w_edge_out,
    w_node_in,
    w_node_out,
    node_cot,
    edge_cot,
):
    slot_rows, asked = fetch(wanted_rows.reshape(NB, 1, 128), nodes)
    new_nodes, new_edges, edge_grad, node_part, slot_grad, total = net(
        nodes,
        edges,
        slot_rows,
        sender_slot.reshape(E // 128, 1, 128),
        receiver.reshape(E // 128, 1, 128),
        w_edge_in,
        w_edge_out,
        w_node_in,
        w_node_out,
        node_cot,
        edge_cot,
    )
    slot_in, out = share(slot_grad, total)
    node_grad, g_ein, g_eout, g_nin, g_nout = finish(slot_in, asked, node_part, out)
    return new_nodes, new_edges, node_grad, edge_grad, g_ein, g_eout, g_nin, g_nout


def solution(mesh):
    split = P(("blk", "grp"), None)
    line = P(("blk", "grp"))
    return jax.shard_map(
        on_device,
        mesh=mesh,
        in_specs=(split, split, split, line, line, P(), P(), P(), P(), split, split),
        out_specs=(split, split, split, split, P(), P(), P(), P()),
        check_vma=False,
    )
```

```python
import functools

import jax
import jax.numpy as jnp
from jax import lax
from jax.experimental import pallas as pl
from jax.experimental.pallas import tpu as pltpu
from jax.sharding import PartitionSpec as P

EPSILON = 1e-05
L = 128
H = 512
NB = 16
NG = 8
GR = 1024
E = 4096
T = 2048
TA = 1024
TB = 1024
EDGE = 4
NODE = 3
F32 = jnp.float32
BF16 = jnp.bfloat16
I16 = jnp.int16
VMEM_LIMIT = 63 * 1024 * 1024
MESH = pl.DeviceIdType.MESH


def mm(a, b):
    return jnp.dot(a, b, preferred_element_type=F32)


def mm_nt(a, b):
    return lax.dot_general(a, b, (((1,), (1,)), ((), ())), preferred_element_type=F32)


def mm_tn(a, b):
    return lax.dot_general(a, b, (((0,), (0,)), ((), ())), preferred_element_type=F32)


def column(rows):
    parts = [
        jnp.transpose(jnp.broadcast_to(rows[i : i + 1, :], (128, 128)))
        for i in range(rows.shape[0])
    ]
    return parts[0] if len(parts) == 1 else jnp.concatenate(parts, axis=0)


def pick(col, width):
    col = col.astype(I16)
    lane = lax.broadcasted_iota(jnp.int32, col.shape, 1).astype(I16)
    one = jnp.ones(col.shape, BF16)
    zero = jnp.zeros(col.shape, BF16)
    return jnp.concatenate(
        [jnp.where(col == lane + I16(128 * j), one, zero) for j in range(width // 128)], axis=1
    )


def spread(rows, width):
    outs = []
    for i in range(rows.shape[0]):
        ids = jnp.broadcast_to(rows[i : i + 1, :], (128, 128)).astype(I16)
        sub = lax.broadcasted_iota(jnp.int32, (128, 128), 0).astype(I16)
        one = jnp.ones((128, 128), BF16)
        zero = jnp.zeros((128, 128), BF16)
        outs.append(
            jnp.concatenate(
                [jnp.where(ids == sub + I16(128 * j), one, zero) for j in range(width // 128)],
                axis=0,
            )
        )
    return outs[0] if len(outs) == 1 else jnp.concatenate(outs, axis=1)


def halves(value, high):
    zero = jnp.zeros_like(value)
    return jnp.concatenate(
        [jnp.where(high, zero, value), jnp.where(high, value, zero)], axis=1
    ).astype(BF16)


def layer_norm(value):
    center = value - jnp.mean(value, axis=-1, keepdims=True)
    inv = lax.rsqrt(jnp.mean(center * center, axis=-1, keepdims=True) + EPSILON)
    return center * inv, inv


def norm_back(upstream, normed, inv):
    first = jnp.mean(upstream, axis=-1, keepdims=True)
    second = jnp.mean(upstream * normed, axis=-1, keepdims=True)
    return (upstream - first - normed * second) * inv


def silu_pair(pre):
    sig = 0.5 * jnp.tanh(0.5 * pre) + 0.5
    hid = pre * sig
    return hid.astype(BF16), sig + hid * (1.0 - sig)


def whole(n):
    return [pl.BlockSpec(memory_space=pltpu.VMEM)] * n


def anywhere(n):
    return [pl.BlockSpec(memory_space=pl.ANY)] * n


def store_block(total, block, value):
    value = value.astype(BF16)
    for half in range(2):
        for i in range(4):
            for j in range(4):
                total[half, 4 * i + j, 16 * block : 16 * block + 16, :] = value[
                    64 * half + 16 * i : 64 * half + 16 * i + 16, 128 * j : 128 * j + 128
                ]


def load_block(out, block, scale):
    lines = []
    for half in range(2):
        for i in range(4):
            lines.append(
                jnp.concatenate(
                    [out[half, 4 * i + j, 16 * block : 16 * block + 16, :] for j in range(4)],
                    axis=1,
                )
            )
    return jnp.concatenate(lines, axis=0).astype(F32) * scale


def remote(src, dst, send, recv, to):
    return pltpu.make_async_remote_copy(
        src_ref=src, dst_ref=dst, send_sem=send, recv_sem=recv, device_id=to, device_id_type=MESH
    )


class Reduce:
    def __init__(self, me, grp, total, out, half_in, mine, piece_in, own, z_in, sems):
        self.me, self.grp = me, grp
        self.core = lax.rem(grp, 2)
        self.zpos = grp // 2
        self.other = (me, grp + 1 - 2 * self.core)
        self.total, self.out, self.half_in, self.mine = total, out, half_in, mine
        self.piece_in, self.own, self.z_in = piece_in, own, z_in
        self.ps, self.pr, self.ls, self.lr = sems

    def pair(self):
        return remote(
            self.total.at[1 - self.core], self.half_in, self.ps.at[0], self.pr.at[0], self.other
        )

    def piece(self, k):
        to = lax.rem(self.me + k, NB)
        return remote(
            self.mine.at[to],
            self.piece_in.at[self.me],
            self.ls.at[0, k],
            self.lr.at[0, k],
            (to, self.grp),
        )

    def along_z(self, k):
        to = lax.rem(self.grp + 2 * k, NG)
        return remote(
            self.own, self.z_in.at[self.zpos], self.ps.at[1 + k], self.pr.at[1 + k], (self.me, to)
        )

    def spread(self, k):
        to = lax.rem(self.me + k, NB)
        place = self.out.at[self.core, self.me]
        return remote(place, place, self.ls.at[1, k], self.lr.at[1, k], (to, self.grp))

    def last(self):
        place = self.out.at[self.core]
        return remote(place, place, self.ps.at[1], self.pr.at[1], self.other)

    def start(self):
        self.pair().start()

    def to_line(self):
        self.pair().wait()
        self.mine[...] = (
            self.total[self.core].astype(F32) + self.half_in[...].astype(F32)
        ).astype(BF16)
        for k in range(1, NB):
            self.piece(k).start()
        self.piece_in[self.me] = self.mine[self.me]

    def to_z(self):
        for k in range(1, NB):
            self.piece(k).wait()
        acc = self.piece_in[0].astype(F32)
        for q in range(1, NB):
            acc = acc + self.piece_in[q].astype(F32)
        self.own[...] = acc.astype(BF16)
        for k in range(1, 4):
            self.along_z(k).start()
        self.z_in[self.zpos] = self.own[...]

    def to_all(self):
        for k in range(1, 4):
            self.along_z(k).wait()
        acc = self.z_in[0].astype(F32)
        for q in range(1, 4):
            acc = acc + self.z_in[q].astype(F32)
        self.out[self.core, self.me] = acc.astype(BF16)
        for k in range(1, NB):
            self.spread(k).start()

    def to_pair(self):
        for k in range(1, NB):
            self.spread(k).wait()
        self.last().start()

    def end(self):
        self.last().wait()


def main_kernel(
    node_scale,
    wanted,
    slot,
    receiver,
    nodes,
    edges_h,
    w_ein_h,
    w_eout_h,
    w_nin_h,
    w_nout_h,
    node_cot_h,
    edge_cot_h,
    new_nodes_h,
    new_edges_h,
    edge_grad_h,
    node_grad_h,
    g_nin_h,
    g_nout_h,
    out_e,
    w_ein,
    w_eout,
    w_nin,
    w_nout,
    node_cot,
    edge_cot,
    asked,
    staged,
    rows_in,
    recv_col,
    send_col,
    pick_recv,
    pick_send,
    spread_recv,
    stacked,
    big,
    hidden,
    slope,
    d_out_all,
    slots2,
    nodes2,
    acc_node,
    acc_slot,
    node_part,
    new_nodes,
    new_edges,
    slot_grad,
    slot_in,
    g_nin,
    g_nout,
    total_n,
    out_n,
    half_n,
    mine_n,
    piece_n,
    own_n,
    z_n,
    total_e,
    half_e,
    mine_e,
    piece_e,
    own_e,
    z_e,
    load_sem,
    store_sem,
    s1,
    r1,
    s2,
    r2,
    s3,
    r3,
    n_ps,
    n_pr,
    n_ls,
    n_lr,
    e_ps,
    e_pr,
    e_ls,
    e_lr,
):
    me = lax.axis_index("blk")
    grp = lax.axis_index("grp")
    barrier = pltpu.get_barrier_semaphore()
    greeted = [(lax.rem(me + k, NB), grp) for k in range(1, NB)]
    greeted += [(me, lax.rem(grp + 2 * k, NG)) for k in range(1, 4)]
    greeted += [(me, grp + 1 - 2 * lax.rem(grp, 2))]
    for peer in greeted:
        pl.semaphore_signal(barrier, inc=1, device_id=peer, device_id_type=MESH)

    loads = [
        pltpu.make_async_copy(src, dst, load_sem.at[i])
        for i, (src, dst) in enumerate(
            [
                (edges_h, stacked.at[:, pl.ds(0, L)]),
                (w_ein_h, w_ein),
                (w_eout_h, w_eout),
                (w_nin_h, w_nin),
                (w_nout_h, w_nout),
                (node_cot_h, node_cot),
                (edge_cot_h, edge_cot),
            ]
        )
    ]
    for copy in loads:
        copy.start()

    red_n = Reduce(
        me, grp, total_n, out_n, half_n, mine_n, piece_n, own_n, z_n, (n_ps, n_pr, n_ls, n_lr)
    )
    red_e = Reduce(
        me, grp, total_e, out_e, half_e, mine_e, piece_e, own_e, z_e, (e_ps, e_pr, e_ls, e_lr)
    )

    def ask(k):
        to = lax.rem(me + k, NB)
        return remote(wanted.at[to], asked.at[me], s1.at[k], r1.at[k], (to, grp))

    def give(k):
        to = lax.rem(me + NB - k, NB)
        return remote(staged.at[k], rows_in.at[me], s2.at[k], r2.at[k], (to, grp))

    def give_slot(k):
        to = lax.rem(me + k, NB)
        return remote(slot_grad.at[to], slot_in.at[me], s3.at[k], r3.at[k], (to, grp))

    nodes2[:, :L] = nodes[: GR // 2, :]
    nodes2[:, L:] = nodes[GR // 2 :, :]

    def place(t, size):
        return pl.ds(pl.multiple_of(t * size, size), size)

    def recv_hot(t, carry):
        rows = place(t, TA)
        ids = receiver[pl.ds(t * (TA // 128), TA // 128)].reshape(TA // 128, 128)
        col = column(ids)
        recv_col[rows, :] = col
        hot = pick(col & 511, 512)
        pick_recv[rows, :] = hot
        both = mm(hot, nodes2[...])
        stacked[rows, 2 * L :] = jnp.where(col >= 512, both[:, L:], both[:, :L]).astype(BF16)
        return carry

    lax.fori_loop(0, E // TA, recv_hot, 0)

    pl.semaphore_wait(barrier, len(greeted))
    for k in range(1, NB):
        ask(k).start()
    asked[me] = wanted[me]

    def send_hot(t, carry):
        rows = place(t, TA)
        ids = slot[pl.ds(t * (TA // 128), TA // 128)].reshape(TA // 128, 128)
        col = column(ids)
        send_col[rows, :] = col
        pick_send[rows, :] = pick(col & 1023, 1024)
        return carry

    lax.fori_loop(0, E // TA, send_hot, 0)
    rows_in[me] = mm(pick(column(asked[me]), GR), nodes[...]).astype(BF16)

    def answer(k, carry):
        ask(k).wait_recv()
        src = lax.rem(me + NB - k, NB)
        staged[k] = mm(pick(column(asked[src]), GR), nodes[...]).astype(BF16)
        give(k).start()
        return carry

    lax.fori_loop(1, NB, answer, 0)
    for copy in loads:
        copy.wait()

    def part_pre(t, carry):
        rows = place(t, T)
        both = jnp.concatenate([stacked[rows, :L], stacked[rows, 2 * L :]], axis=1)
        weight = jnp.concatenate([w_ein[:L, :], w_ein[2 * L :, :]], axis=0)
        big[rows, :] = mm(both, weight)
        return carry

    lax.fori_loop(0, E // T, part_pre, 0)

    def recv_spread(t, carry):
        ids = receiver[pl.ds(t * (TA // 128), TA // 128)].reshape(TA // 128, 128)
        spread_recv[t] = spread(ids & 511, 512)
        return carry

    lax.fori_loop(0, E // TA, recv_spread, 0)
    acc_node[...] = jnp.zeros_like(acc_node)
    acc_slot[...] = jnp.zeros_like(acc_slot)

    for k in range(1, NB):
        ask(k).wait_send()
        give(k).wait()
    for p in range(8):
        slots2[128 * p : 128 * p + 128, :L] = rows_in[p]
        slots2[128 * p : 128 * p + 128, L:] = rows_in[p + 8]

    def forward(t, carry):
        rows = place(t, T)
        both = mm(pick_send[rows, :], slots2[...])
        high = send_col[rows, :] >= 1024
        send_rows = jnp.where(high, both[:, L:], both[:, :L]).astype(BF16)
        stacked[rows, L : 2 * L] = send_rows
        pre = big[rows, :] + mm(send_rows, w_ein[L : 2 * L, :])
        hid, slp = silu_pair(pre)
        hidden[rows, :] = hid
        slope[rows, :] = slp.astype(BF16)
        norm, inv = layer_norm(mm(hid, w_eout[...]))
        big[rows, :L] = norm
        big[rows, L : 2 * L] = jnp.broadcast_to(inv, (T, L))
        message = norm.astype(BF16).astype(F32)
        new_edges[rows, :] = (stacked[rows, :L].astype(F32) + message).astype(BF16)
        values = halves(message, recv_col[rows, :] >= 512)
        for i in range(T // TA):
            acc_node[...] += mm(spread_recv[t * (T // TA) + i], values[TA * i : TA * i + TA])
        return carry

    lax.fori_loop(0, E // T, forward, 0)
    stores = [pltpu.make_async_copy(new_edges, new_edges_h, store_sem.at[0])]
    stores[0].start()

    inbound = jnp.concatenate([acc_node[:, :L], acc_node[:, L:]], axis=0).astype(BF16)
    node = nodes[...]
    node_input = jnp.concatenate([node, inbound], axis=1)
    hid, slp = silu_pair(mm(node_input, w_nin[...]))
    norm, inv = layer_norm(mm(hid, w_nout[...]))
    new_nodes[...] = (node.astype(F32) + norm).astype(BF16)
    stores.append(pltpu.make_async_copy(new_nodes, new_nodes_h, store_sem.at[1]))
    stores[1].start()
    cot = node_cot[...].astype(F32)
    d_out = norm_back(cot, norm, inv).astype(BF16)
    d_pre = (mm_nt(d_out, w_nout[...]) * slp).astype(BF16)
    d_in = mm_nt(d_pre, w_nin[...])
    node_part[...] = cot + d_in[:, :L]
    d_inbound = d_in[:, L:].astype(BF16)
    nodes2[:, :L] = d_inbound[: GR // 2, :]
    nodes2[:, L:] = d_inbound[GR // 2 :, :]
    store_block(total_n, 2, mm_tn(d_out, hid))
    g_in = mm_tn(node_input, d_pre)
    store_block(total_n, 0, g_in[:128])
    store_block(total_n, 1, g_in[128:])
    acc_node[...] = jnp.zeros_like(acc_node)
    red_n.start()

    def backward(t, carry):
        rows = place(t, T)
        both = mm(pick_recv[rows, :], nodes2[...])
        cot = edge_cot[rows, :].astype(F32)
        upstream = cot + jnp.where(recv_col[rows, :] >= 512, both[:, L:], both[:, :L])
        d_out = norm_back(upstream, big[rows, :L], big[rows, L : 2 * L]).astype(BF16)
        d_out_all[rows, :] = d_out
        d_pre = (mm_nt(d_out, w_eout[...]) * slope[rows, :].astype(F32)).astype(BF16)
        slope[rows, :] = d_pre

        @pl.when(t == 0)
        def _():
            red_n.to_line()

        return carry

    lax.fori_loop(0, E // T, backward, 0)
    for b in range(3):
        store_block(total_e, b, mm_tn(stacked[:, 128 * b : 128 * b + 128], slope[...]))
    store_block(total_e, 3, mm_tn(d_out_all[...], hidden[...]))
    red_e.start()
    red_n.to_z()

    def back_input(t, carry):
        rows = place(t, TB)
        d_in = mm_nt(slope[rows, :], w_ein[...])
        big[rows, 2 * L : 3 * L] = edge_cot[rows, :].astype(F32) + d_in[:, :L]
        send = slot[pl.ds(t * (TB // 128), TB // 128)].reshape(TB // 128, 128)
        acc_slot[...] += mm(
            spread(send & 1023, 1024), halves(d_in[:, L : 2 * L], send_col[rows, :] >= 1024)
        )
        acc_node[...] += mm(spread_recv[t], halves(d_in[:, 2 * L :], recv_col[rows, :] >= 512))

        @pl.when(t == 0)
        def _():
            red_e.to_line()

        @pl.when(t == 2)
        def _():
            red_n.to_all()

        return carry

    lax.fori_loop(0, E // TB, back_input, 0)
    for p in range(8):
        slot_grad[p] = acc_slot[128 * p : 128 * p + 128, :L].astype(BF16)
        slot_grad[p + 8] = acc_slot[128 * p : 128 * p + 128, L:].astype(BF16)
    for k in range(1, NB):
        give_slot(k).start()
    slot_in[me] = slot_grad[me]
    stores.append(
        pltpu.make_async_copy(big.at[:, pl.ds(2 * L, L)], edge_grad_h, store_sem.at[2])
    )
    stores[2].start()
    red_e.to_z()
    node_part[: GR // 2, :] += acc_node[:, :L]
    node_part[GR // 2 :, :] += acc_node[:, L:]
    red_n.to_pair()
    red_e.to_all()
    red_n.end()
    for b in range(2):
        g_nin[128 * b : 128 * b + 128, :] = load_block(out_n, b, node_scale)
    g_nout[...] = jnp.transpose(load_block(out_n, 2, node_scale))
    stores.append(pltpu.make_async_copy(g_nin, g_nin_h, store_sem.at[3]))
    stores.append(pltpu.make_async_copy(g_nout, g_nout_h, store_sem.at[4]))
    stores[3].start()
    stores[4].start()
    for k in range(1, NB):
        give_slot(k).wait()

    def home(q, carry):
        node_part[...] += mm(spread(asked[q], GR), slot_in[q])
        return carry

    lax.fori_loop(0, NB, home, 0)
    stores.append(pltpu.make_async_copy(node_part, node_grad_h, store_sem.at[5]))
    stores[5].start()
    red_e.to_pair()
    red_e.end()
    for copy in stores:
        copy.wait()


def main(*args):
    sem = pltpu.SemaphoreType.DMA
    vm = pltpu.VMEM

    def reduce_buffers(blocks, with_out):
        rows = 16 * blocks
        out = [vm((2, NB, rows, L), BF16)] * (2 if with_out else 1)
        return out + [
            vm((NB, rows, L), BF16),
            vm((NB, rows, L), BF16),
            vm((NB, rows, L), BF16),
            vm((rows, L), BF16),
            vm((4, rows, L), BF16),
        ]

    return pl.pallas_call(
        functools.partial(main_kernel, float((GR * NB * NG) ** -0.5)),
        name="message_passing",
        out_shape=(
            jax.ShapeDtypeStruct((GR, L), BF16),
            jax.ShapeDtypeStruct((E, L), BF16),
            jax.ShapeDtypeStruct((E, L), F32),
            jax.ShapeDtypeStruct((GR, L), F32),
            jax.ShapeDtypeStruct((2 * L, H), F32),
            jax.ShapeDtypeStruct((H, L), F32),
            jax.ShapeDtypeStruct((2, NB, 16 * EDGE, L), BF16),
        ),
        in_specs=whole(4) + anywhere(7),
        out_specs=anywhere(6) + whole(1),
        scratch_shapes=[
            vm((3 * L, H), BF16),
            vm((H, L), BF16),
            vm((2 * L, H), BF16),
            vm((H, L), BF16),
            vm((GR, L), BF16),
            vm((E, L), BF16),
            vm((NB, 1, 128), jnp.int32),
            vm((NB, 128, L), BF16),
            vm((NB, 128, L), BF16),
            vm((E, L), jnp.int32),
            vm((E, L), jnp.int32),
            vm((E, 512), BF16),
            vm((E, 1024), BF16),
            vm((E // TA, 512, TA), BF16),
            vm((E, 3 * L), BF16),
            vm((E, H), F32),
            vm((E, H), BF16),
            vm((E, H), BF16),
            vm((E, L), BF16),
            vm((GR, 2 * L), BF16),
            vm((GR // 2, 2 * L), BF16),
            vm((GR // 2, 2 * L), F32),
            vm((GR, 2 * L), F32),
            vm((GR, L), F32),
            vm((GR, L), BF16),
            vm((E, L), BF16),
            vm((NB, 128, L), BF16),
            vm((NB, 128, L), BF16),
            vm((2 * L, H), F32),
            vm((H, L), F32),
        ]
        + reduce_buffers(NODE, True)
        + reduce_buffers(EDGE, False)
        + [sem((7,)), sem((6,))]
        + [sem((NB,))] * 6
        + [sem((5,)), sem((5,)), sem((2, NB)), sem((2, NB))] * 2,
        compiler_params=pltpu.CompilerParams(
            collective_id=0, has_side_effects=True, vmem_limit_bytes=VMEM_LIMIT
        ),
    )(*args)


def finish_kernel(
    edge_scale, out, a0, a1, a2, a3, a4, a5, o0, o1, o2, o3, o4, o5, g_ein, g_eout, sems
):
    copies = [
        pltpu.make_async_copy(src, dst, sems.at[i])
        for i, (src, dst) in enumerate(zip((a0, a1, a2, a3, a4, a5), (o0, o1, o2, o3, o4, o5)))
    ]
    for copy in copies:
        copy.start()
    for b in range(3):
        g_ein[128 * b : 128 * b + 128, :] = load_block(out, b, edge_scale)
    g_eout[...] = jnp.transpose(load_block(out, 3, edge_scale))
    for copy in copies:
        copy.wait()


def finish(out, *arrays):
    return pl.pallas_call(
        functools.partial(finish_kernel, float((E * NB * NG) ** -0.5)),
        name="finish",
        out_shape=tuple(jax.ShapeDtypeStruct(a.shape, a.dtype) for a in arrays)
        + (
            jax.ShapeDtypeStruct((3 * L, H), F32),
            jax.ShapeDtypeStruct((H, L), F32),
        ),
        in_specs=whole(1) + anywhere(6),
        out_specs=anywhere(6) + whole(2),
        scratch_shapes=[pltpu.SemaphoreType.DMA((6,))],
        compiler_params=pltpu.CompilerParams(vmem_limit_bytes=VMEM_LIMIT),
    )(out, *arrays)


def on_device(
    nodes,
    edges,
    wanted_rows,
    sender_slot,
    receiver,
    w_edge_in,
    w_edge_out,
    w_node_in,
    w_node_out,
    node_cot,
    edge_cot,
):
    *arrays, out = main(
        wanted_rows.reshape(NB, 1, 128),
        sender_slot.reshape(E // 128, 1, 128),
        receiver.reshape(E // 128, 1, 128),
        nodes,
        edges,
        w_edge_in,
        w_edge_out,
        w_node_in,
        w_node_out,
        node_cot,
        edge_cot,
    )
    new_nodes, new_edges, edge_grad, node_grad, g_nin, g_nout, g_ein, g_eout = finish(out, *arrays)
    return new_nodes, new_edges, node_grad, edge_grad, g_ein, g_eout, g_nin, g_nout


def solution(mesh):
    split = P(("blk", "grp"), None)
    line = P(("blk", "grp"))
    return jax.shard_map(
        on_device,
        mesh=mesh,
        in_specs=(split, split, split, line, line, P(), P(), P(), P(), split, split),
        out_specs=(split, split, split, split, P(), P(), P(), P()),
        check_vma=False,
    )
```

```python
import functools

import jax
import jax.numpy as jnp
from jax import lax
from jax.experimental import pallas as pl
from jax.experimental.pallas import tpu as pltpu
from jax.sharding import PartitionSpec as P

EPSILON = 1e-05
L = 128
H = 512
NB = 16
NG = 8
GR = 1024
E = 4096
T = 2048
TA = 1024
TB = 1024
EDGE = 4
NODE = 3
F32 = jnp.float32
BF16 = jnp.bfloat16
I16 = jnp.int16
VMEM_LIMIT = 63 * 1024 * 1024
MESH = pl.DeviceIdType.MESH


def mm(a, b):
    return jnp.dot(a, b, preferred_element_type=F32)


def mm_nt(a, b):
    return lax.dot_general(a, b, (((1,), (1,)), ((), ())), preferred_element_type=F32)


def mm_tn(a, b):
    return lax.dot_general(a, b, (((0,), (0,)), ((), ())), preferred_element_type=F32)


def column(rows):
    parts = [
        jnp.transpose(jnp.broadcast_to(rows[i : i + 1, :], (128, 128)))
        for i in range(rows.shape[0])
    ]
    return parts[0] if len(parts) == 1 else jnp.concatenate(parts, axis=0)


def pick(col, width):
    col = col.astype(I16)
    lane = lax.broadcasted_iota(jnp.int32, col.shape, 1).astype(I16)
    one = jnp.ones(col.shape, BF16)
    zero = jnp.zeros(col.shape, BF16)
    return jnp.concatenate(
        [jnp.where(col == lane + I16(128 * j), one, zero) for j in range(width // 128)], axis=1
    )


def spread(rows, width):
    outs = []
    for i in range(rows.shape[0]):
        ids = jnp.broadcast_to(rows[i : i + 1, :], (128, 128)).astype(I16)
        sub = lax.broadcasted_iota(jnp.int32, (128, 128), 0).astype(I16)
        one = jnp.ones((128, 128), BF16)
        zero = jnp.zeros((128, 128), BF16)
        outs.append(
            jnp.concatenate(
                [jnp.where(ids == sub + I16(128 * j), one, zero) for j in range(width // 128)],
                axis=0,
            )
        )
    return outs[0] if len(outs) == 1 else jnp.concatenate(outs, axis=1)


def halves(value, high):
    zero = jnp.zeros_like(value)
    return jnp.concatenate(
        [jnp.where(high, zero, value), jnp.where(high, value, zero)], axis=1
    ).astype(BF16)


def layer_norm(value):
    center = value - jnp.mean(value, axis=-1, keepdims=True)
    inv = lax.rsqrt(jnp.mean(center * center, axis=-1, keepdims=True) + EPSILON)
    return center * inv, inv


def norm_back(upstream, normed, inv):
    first = jnp.mean(upstream, axis=-1, keepdims=True)
    second = jnp.mean(upstream * normed, axis=-1, keepdims=True)
    return (upstream - first - normed * second) * inv


def silu_pair(pre):
    sig = 0.5 * jnp.tanh(0.5 * pre) + 0.5
    hid = pre * sig
    return hid.astype(BF16), sig + hid * (1.0 - sig)


def whole(n):
    return [pl.BlockSpec(memory_space=pltpu.VMEM)] * n


def anywhere(n):
    return [pl.BlockSpec(memory_space=pl.ANY)] * n


def store_block(total, block, value):
    value = value.astype(BF16)
    for half in range(2):
        for i in range(4):
            for j in range(4):
                total[half, 4 * i + j, 16 * block : 16 * block + 16, :] = value[
                    64 * half + 16 * i : 64 * half + 16 * i + 16, 128 * j : 128 * j + 128
                ]


def load_block(out, block, scale):
    lines = []
    for half in range(2):
        for i in range(4):
            lines.append(
                jnp.concatenate(
                    [out[half, 4 * i + j, 16 * block : 16 * block + 16, :] for j in range(4)],
                    axis=1,
                )
            )
    return jnp.concatenate(lines, axis=0).astype(F32) * scale


def remote(src, dst, send, recv, to):
    return pltpu.make_async_remote_copy(
        src_ref=src, dst_ref=dst, send_sem=send, recv_sem=recv, device_id=to, device_id_type=MESH
    )


class Reduce:
    def __init__(self, me, grp, total, out, half_in, mine, piece_in, own, z_in, sems):
        self.me, self.grp = me, grp
        self.core = lax.rem(grp, 2)
        self.zpos = grp // 2
        self.other = (me, grp + 1 - 2 * self.core)
        self.total, self.out, self.half_in, self.mine = total, out, half_in, mine
        self.piece_in, self.own, self.z_in = piece_in, own, z_in
        self.ps, self.pr, self.ls, self.lr = sems

    def pair(self):
        return remote(
            self.total.at[1 - self.core], self.half_in, self.ps.at[0], self.pr.at[0], self.other
        )

    def piece(self, k):
        to = lax.rem(self.me + k, NB)
        return remote(
            self.mine.at[to],
            self.piece_in.at[self.me],
            self.ls.at[0, k],
            self.lr.at[0, k],
            (to, self.grp),
        )

    def along_z(self, k):
        to = lax.rem(self.grp + 2 * k, NG)
        return remote(
            self.own, self.z_in.at[self.zpos], self.ps.at[1 + k], self.pr.at[1 + k], (self.me, to)
        )

    def spread(self, k):
        to = lax.rem(self.me + k, NB)
        place = self.out.at[self.core, self.me]
        return remote(place, place, self.ls.at[1, k], self.lr.at[1, k], (to, self.grp))

    def last(self):
        place = self.out.at[self.core]
        return remote(place, place, self.ps.at[1], self.pr.at[1], self.other)

    def start(self):
        self.pair().start()

    def to_line(self):
        self.pair().wait()
        self.mine[...] = (
            self.total[self.core].astype(F32) + self.half_in[...].astype(F32)
        ).astype(BF16)
        for k in range(1, NB):
            self.piece(k).start()
        self.piece_in[self.me] = self.mine[self.me]

    def to_z(self):
        for k in range(1, NB):
            self.piece(k).wait()
        acc = self.piece_in[0].astype(F32)
        for q in range(1, NB):
            acc = acc + self.piece_in[q].astype(F32)
        self.own[...] = acc.astype(BF16)
        for k in range(1, 4):
            self.along_z(k).start()
        self.z_in[self.zpos] = self.own[...]

    def to_all(self):
        for k in range(1, 4):
            self.along_z(k).wait()
        acc = self.z_in[0].astype(F32)
        for q in range(1, 4):
            acc = acc + self.z_in[q].astype(F32)
        self.out[self.core, self.me] = acc.astype(BF16)
        for k in range(1, NB):
            self.spread(k).start()

    def to_pair(self):
        for k in range(1, NB):
            self.spread(k).wait()
        self.last().start()

    def end(self):
        self.last().wait()


def main_kernel(
    node_scale,
    wanted,
    slot,
    receiver,
    nodes,
    edges_h,
    w_ein_h,
    w_eout_h,
    w_nin_h,
    w_nout_h,
    node_cot_h,
    edge_cot_h,
    new_nodes_h,
    new_edges_h,
    edge_grad_h,
    node_grad_h,
    g_nin_h,
    g_nout_h,
    out_e,
    w_ein,
    w_eout,
    w_nin,
    w_nout,
    node_cot,
    edge_cot,
    asked,
    staged,
    rows_in,
    recv_col,
    send_col,
    pick_recv,
    pick_send,
    spread_recv,
    stacked,
    big,
    hidden,
    slope,
    d_out_all,
    slots2,
    nodes2,
    acc_node,
    acc_slot,
    node_part,
    new_nodes,
    new_edges,
    slot_grad,
    slot_in,
    g_nin,
    g_nout,
    total_n,
    out_n,
    half_n,
    mine_n,
    piece_n,
    own_n,
    z_n,
    total_e,
    half_e,
    mine_e,
    piece_e,
    own_e,
    z_e,
    load_sem,
    store_sem,
    s1,
    r1,
    s2,
    r2,
    s3,
    r3,
    n_ps,
    n_pr,
    n_ls,
    n_lr,
    e_ps,
    e_pr,
    e_ls,
    e_lr,
):
    me = lax.axis_index("blk")
    grp = lax.axis_index("grp")
    barrier = pltpu.get_barrier_semaphore()
    greeted = [(lax.rem(me + k, NB), grp) for k in range(1, NB)]
    greeted += [(me, lax.rem(grp + 2 * k, NG)) for k in range(1, 4)]
    greeted += [(me, grp + 1 - 2 * lax.rem(grp, 2))]
    for peer in greeted:
        pl.semaphore_signal(barrier, inc=1, device_id=peer, device_id_type=MESH)

    loads = [
        pltpu.make_async_copy(src, dst, load_sem.at[i])
        for i, (src, dst) in enumerate(
            [
                (edges_h, stacked.at[:, pl.ds(0, L)]),
                (w_ein_h, w_ein),
                (w_eout_h, w_eout),
                (w_nin_h, w_nin),
                (w_nout_h, w_nout),
                (node_cot_h, node_cot),
                (edge_cot_h, edge_cot),
            ]
        )
    ]
    for copy in loads:
        copy.start()

    red_n = Reduce(
        me, grp, total_n, out_n, half_n, mine_n, piece_n, own_n, z_n, (n_ps, n_pr, n_ls, n_lr)
    )
    red_e = Reduce(
        me, grp, total_e, out_e, half_e, mine_e, piece_e, own_e, z_e, (e_ps, e_pr, e_ls, e_lr)
    )

    def ask(k):
        to = lax.rem(me + k, NB)
        return remote(wanted.at[to], asked.at[me], s1.at[k], r1.at[k], (to, grp))

    def give(k):
        to = lax.rem(me + NB - k, NB)
        return remote(staged.at[k], rows_in.at[me], s2.at[k], r2.at[k], (to, grp))

    def give_slot(k):
        to = lax.rem(me + k, NB)
        return remote(slot_grad.at[to], slot_in.at[me], s3.at[k], r3.at[k], (to, grp))

    nodes2[:, :L] = nodes[: GR // 2, :]
    nodes2[:, L:] = nodes[GR // 2 :, :]

    def place(t, size):
        return pl.ds(pl.multiple_of(t * size, size), size)

    def recv_hot(t, carry):
        rows = place(t, TA)
        ids = receiver[pl.ds(t * (TA // 128), TA // 128)].reshape(TA // 128, 128)
        col = column(ids)
        recv_col[rows, :] = col
        hot = pick(col & 511, 512)
        pick_recv[rows, :] = hot
        both = mm(hot, nodes2[...])
        stacked[rows, 2 * L :] = jnp.where(col >= 512, both[:, L:], both[:, :L]).astype(BF16)
        return carry

    lax.fori_loop(0, E // TA, recv_hot, 0)

    pl.semaphore_wait(barrier, len(greeted))
    for k in range(1, NB):
        ask(k).start()
    asked[me] = wanted[me]

    def send_hot(t, carry):
        rows = place(t, TA)
        ids = slot[pl.ds(t * (TA // 128), TA // 128)].reshape(TA // 128, 128)
        col = column(ids)
        send_col[rows, :] = col
        pick_send[rows, :] = pick(col & 1023, 1024)
        return carry

    lax.fori_loop(0, E // TA, send_hot, 0)
    rows_in[me] = mm(pick(column(asked[me]), GR), nodes[...]).astype(BF16)

    def answer(k, carry):
        ask(k).wait_recv()
        src = lax.rem(me + NB - k, NB)
        staged[k] = mm(pick(column(asked[src]), GR), nodes[...]).astype(BF16)
        give(k).start()
        return carry

    lax.fori_loop(1, NB, answer, 0)
    for copy in loads:
        copy.wait()

    def part_pre(t, carry):
        rows = place(t, T)
        both = jnp.concatenate([stacked[rows, :L], stacked[rows, 2 * L :]], axis=1)
        weight = jnp.concatenate([w_ein[:L, :], w_ein[2 * L :, :]], axis=0)
        big[rows, :] = mm(both, weight)
        return carry

    lax.fori_loop(0, E // T, part_pre, 0)

    def recv_spread(t, carry):
        ids = receiver[pl.ds(t * (TA // 128), TA // 128)].reshape(TA // 128, 128)
        spread_recv[t] = spread(ids & 511, 512)
        return carry

    lax.fori_loop(0, E // TA, recv_spread, 0)
    acc_node[...] = jnp.zeros_like(acc_node)
    acc_slot[...] = jnp.zeros_like(acc_slot)

    for k in range(1, NB):
        ask(k).wait_send()
        give(k).wait()
    for p in range(8):
        slots2[128 * p : 128 * p + 128, :L] = rows_in[p]
        slots2[128 * p : 128 * p + 128, L:] = rows_in[p + 8]

    def forward(t, carry):
        rows = place(t, T)
        both = mm(pick_send[rows, :], slots2[...])
        high = send_col[rows, :] >= 1024
        send_rows = jnp.where(high, both[:, L:], both[:, :L]).astype(BF16)
        stacked[rows, L : 2 * L] = send_rows
        pre = big[rows, :] + mm(send_rows, w_ein[L : 2 * L, :])
        hid, slp = silu_pair(pre)
        hidden[rows, :] = hid
        slope[rows, :] = slp.astype(BF16)
        norm, inv = layer_norm(mm(hid, w_eout[...]))
        big[rows, :L] = norm
        big[rows, L : 2 * L] = jnp.broadcast_to(inv, (T, L))
        message = norm.astype(BF16).astype(F32)
        new_edges[rows, :] = (stacked[rows, :L].astype(F32) + message).astype(BF16)
        values = halves(message, recv_col[rows, :] >= 512)
        for i in range(T // TA):
            acc_node[...] += mm(spread_recv[t * (T // TA) + i], values[TA * i : TA * i + TA])
        return carry

    lax.fori_loop(0, E // T, forward, 0)
    stores = [pltpu.make_async_copy(new_edges, new_edges_h, store_sem.at[0])]
    stores[0].start()

    inbound = jnp.concatenate([acc_node[:, :L], acc_node[:, L:]], axis=0).astype(BF16)
    node = nodes[...]
    node_input = jnp.concatenate([node, inbound], axis=1)
    hid, slp = silu_pair(mm(node_input, w_nin[...]))
    norm, inv = layer_norm(mm(hid, w_nout[...]))
    new_nodes[...] = (node.astype(F32) + norm).astype(BF16)
    stores.append(pltpu.make_async_copy(new_nodes, new_nodes_h, store_sem.at[1]))
    stores[1].start()
    cot = node_cot[...].astype(F32)
    d_out = norm_back(cot, norm, inv).astype(BF16)
    d_pre = (mm_nt(d_out, w_nout[...]) * slp).astype(BF16)
    d_in = mm_nt(d_pre, w_nin[...])
    node_part[...] = cot + d_in[:, :L]
    d_inbound = d_in[:, L:].astype(BF16)
    nodes2[:, :L] = d_inbound[: GR // 2, :]
    nodes2[:, L:] = d_inbound[GR // 2 :, :]
    store_block(total_n, 2, mm_tn(d_out, hid))
    g_in = mm_tn(node_input, d_pre)
    store_block(total_n, 0, g_in[:128])
    store_block(total_n, 1, g_in[128:])
    acc_node[...] = jnp.zeros_like(acc_node)
    red_n.start()

    def backward(t, carry):
        rows = place(t, T)
        both = mm(pick_recv[rows, :], nodes2[...])
        cot = edge_cot[rows, :].astype(F32)
        upstream = cot + jnp.where(recv_col[rows, :] >= 512, both[:, L:], both[:, :L])
        d_out = norm_back(upstream, big[rows, :L], big[rows, L : 2 * L]).astype(BF16)
        d_out_all[rows, :] = d_out
        d_pre = (mm_nt(d_out, w_eout[...]) * slope[rows, :].astype(F32)).astype(BF16)
        slope[rows, :] = d_pre

        @pl.when(t == 0)
        def _():
            red_n.to_line()

        return carry

    lax.fori_loop(0, E // T, backward, 0)
    for b in range(3):
        store_block(total_e, b, mm_tn(stacked[:, 128 * b : 128 * b + 128], slope[...]))
    store_block(total_e, 3, mm_tn(d_out_all[...], hidden[...]))
    red_e.start()
    red_n.to_z()

    def back_input(t, carry):
        rows = place(t, TB)
        d_in = mm_nt(slope[rows, :], w_ein[...])
        big[rows, 2 * L : 3 * L] = edge_cot[rows, :].astype(F32) + d_in[:, :L]
        send = slot[pl.ds(t * (TB // 128), TB // 128)].reshape(TB // 128, 128)
        acc_slot[...] += mm(
            spread(send & 1023, 1024), halves(d_in[:, L : 2 * L], send_col[rows, :] >= 1024)
        )
        acc_node[...] += mm(spread_recv[t], halves(d_in[:, 2 * L :], recv_col[rows, :] >= 512))

        @pl.when(t == 0)
        def _():
            red_e.to_line()

        @pl.when(t == 2)
        def _():
            red_n.to_all()

        return carry

    lax.fori_loop(0, E // TB, back_input, 0)
    for p in range(8):
        slot_grad[p] = acc_slot[128 * p : 128 * p + 128, :L].astype(BF16)
        slot_grad[p + 8] = acc_slot[128 * p : 128 * p + 128, L:].astype(BF16)
    for k in range(1, NB):
        give_slot(k).start()
    slot_in[me] = slot_grad[me]
    stores.append(
        pltpu.make_async_copy(big.at[:, pl.ds(2 * L, L)], edge_grad_h, store_sem.at[2])
    )
    stores[2].start()
    red_e.to_z()
    node_part[: GR // 2, :] += acc_node[:, :L]
    node_part[GR // 2 :, :] += acc_node[:, L:]
    red_n.to_pair()
    red_e.to_all()
    red_n.end()
    for b in range(2):
        g_nin[128 * b : 128 * b + 128, :] = load_block(out_n, b, node_scale)
    g_nout[...] = jnp.transpose(load_block(out_n, 2, node_scale))
    stores.append(pltpu.make_async_copy(g_nin, g_nin_h, store_sem.at[3]))
    stores.append(pltpu.make_async_copy(g_nout, g_nout_h, store_sem.at[4]))
    stores[3].start()
    stores[4].start()
    for k in range(1, NB):
        give_slot(k).wait()

    def home(q, carry):
        node_part[...] += mm(spread(asked[q], GR), slot_in[q])
        return carry

    lax.fori_loop(0, NB, home, 0)
    stores.append(pltpu.make_async_copy(node_part, node_grad_h, store_sem.at[5]))
    stores[5].start()
    red_e.to_pair()
    red_e.end()
    for copy in stores:
        copy.wait()


def main(*args):
    sem = pltpu.SemaphoreType.DMA
    vm = pltpu.VMEM

    def reduce_buffers(blocks, with_out):
        rows = 16 * blocks
        out = [vm((2, NB, rows, L), BF16)] * (2 if with_out else 1)
        return out + [
            vm((NB, rows, L), BF16),
            vm((NB, rows, L), BF16),
            vm((NB, rows, L), BF16),
            vm((rows, L), BF16),
            vm((4, rows, L), BF16),
        ]

    return pl.pallas_call(
        functools.partial(main_kernel, float((GR * NB * NG) ** -0.5)),
        name="message_passing",
        out_shape=(
            jax.ShapeDtypeStruct((GR, L), BF16),
            jax.ShapeDtypeStruct((E, L), BF16),
            jax.ShapeDtypeStruct((E, L), F32),
            jax.ShapeDtypeStruct((GR, L), F32),
            jax.ShapeDtypeStruct((2 * L, H), F32),
            jax.ShapeDtypeStruct((H, L), F32),
            jax.ShapeDtypeStruct((2, NB, 16 * EDGE, L), BF16),
        ),
        in_specs=whole(4) + anywhere(7),
        out_specs=anywhere(6) + whole(1),
        scratch_shapes=[
            vm((3 * L, H), BF16),
            vm((H, L), BF16),
            vm((2 * L, H), BF16),
            vm((H, L), BF16),
            vm((GR, L), BF16),
            vm((E, L), BF16),
            vm((NB, 1, 128), jnp.int32),
            vm((NB, 128, L), BF16),
            vm((NB, 128, L), BF16),
            vm((E, L), jnp.int32),
            vm((E, L), jnp.int32),
            vm((E, 512), BF16),
            vm((E, 1024), BF16),
            vm((E // TA, 512, TA), BF16),
            vm((E, 3 * L), BF16),
            vm((E, H), F32),
            vm((E, H), BF16),
            vm((E, H), BF16),
            vm((E, L), BF16),
            vm((GR, 2 * L), BF16),
            vm((GR // 2, 2 * L), BF16),
            vm((GR // 2, 2 * L), F32),
            vm((GR, 2 * L), F32),
            vm((GR, L), F32),
            vm((GR, L), BF16),
            vm((E, L), BF16),
            vm((NB, 128, L), BF16),
            vm((NB, 128, L), BF16),
            vm((2 * L, H), F32),
            vm((H, L), F32),
        ]
        + reduce_buffers(NODE, True)
        + reduce_buffers(EDGE, False)
        + [sem((7,)), sem((6,))]
        + [sem((NB,))] * 6
        + [sem((5,)), sem((5,)), sem((2, NB)), sem((2, NB))] * 2,
        compiler_params=pltpu.CompilerParams(
            collective_id=0, has_side_effects=True, vmem_limit_bytes=VMEM_LIMIT
        ),
    )(*args)


def finish_kernel(edge_scale, out, *refs):
    count = 6
    sources, targets = refs[:count], refs[count : 2 * count]
    g_ein, g_eout = refs[2 * count : 2 * count + 2]
    held = refs[2 * count + 2 : 3 * count + 2]
    load_sem, store_sem = refs[3 * count + 2 :]
    loads = [
        pltpu.make_async_copy(sources[i], held[i], load_sem.at[i]) for i in range(count)
    ]
    stores = [
        pltpu.make_async_copy(held[i], targets[i], store_sem.at[i]) for i in range(count)
    ]
    for copy in loads:
        copy.start()
    for load, store in zip(loads, stores):
        load.wait()
        store.start()
    for b in range(3):
        g_ein[128 * b : 128 * b + 128, :] = load_block(out, b, edge_scale)
    g_eout[...] = jnp.transpose(load_block(out, 3, edge_scale))
    for copy in stores:
        copy.wait()


def finish(out, *arrays):
    return pl.pallas_call(
        functools.partial(finish_kernel, float((E * NB * NG) ** -0.5)),
        name="finish",
        out_shape=tuple(jax.ShapeDtypeStruct(a.shape, a.dtype) for a in arrays)
        + (
            jax.ShapeDtypeStruct((3 * L, H), F32),
            jax.ShapeDtypeStruct((H, L), F32),
        ),
        in_specs=whole(1) + anywhere(6),
        out_specs=anywhere(6) + whole(2),
        scratch_shapes=[pltpu.VMEM(a.shape, a.dtype) for a in arrays]
        + [pltpu.SemaphoreType.DMA((6,)), pltpu.SemaphoreType.DMA((6,))],
        compiler_params=pltpu.CompilerParams(vmem_limit_bytes=VMEM_LIMIT),
    )(out, *arrays)


def on_device(
    nodes,
    edges,
    wanted_rows,
    sender_slot,
    receiver,
    w_edge_in,
    w_edge_out,
    w_node_in,
    w_node_out,
    node_cot,
    edge_cot,
):
    *arrays, out = main(
        wanted_rows.reshape(NB, 1, 128),
        sender_slot.reshape(E // 128, 1, 128),
        receiver.reshape(E // 128, 1, 128),
        nodes,
        edges,
        w_edge_in,
        w_edge_out,
        w_node_in,
        w_node_out,
        node_cot,
        edge_cot,
    )
    new_nodes, new_edges, edge_grad, node_grad, g_nin, g_nout, g_ein, g_eout = finish(out, *arrays)
    return new_nodes, new_edges, node_grad, edge_grad, g_ein, g_eout, g_nin, g_nout


def solution(mesh):
    split = P(("blk", "grp"), None)
    line = P(("blk", "grp"))
    return jax.shard_map(
        on_device,
        mesh=mesh,
        in_specs=(split, split, split, line, line, P(), P(), P(), P(), split, split),
        out_specs=(split, split, split, split, P(), P(), P(), P()),
        check_vma=False,
    )
```

```python
import functools

import jax
import jax.numpy as jnp
from jax import lax
from jax.experimental import pallas as pl
from jax.experimental.pallas import tpu as pltpu
from jax.sharding import PartitionSpec as P

EPSILON = 1e-05
L = 128
H = 512
NB = 16
NG = 8
GR = 1024
E = 4096
T = 2048
TA = 1024
TB = 1024
EDGE = 4
NODE = 3
F32 = jnp.float32
BF16 = jnp.bfloat16
I16 = jnp.int16
VMEM_LIMIT = 63 * 1024 * 1024
MESH = pl.DeviceIdType.MESH


def mm(a, b):
    return jnp.dot(a, b, preferred_element_type=F32)


def mm_nt(a, b):
    return lax.dot_general(a, b, (((1,), (1,)), ((), ())), preferred_element_type=F32)


def mm_tn(a, b):
    return lax.dot_general(a, b, (((0,), (0,)), ((), ())), preferred_element_type=F32)


def column(rows):
    parts = [
        jnp.transpose(jnp.broadcast_to(rows[i : i + 1, :], (128, 128)))
        for i in range(rows.shape[0])
    ]
    return parts[0] if len(parts) == 1 else jnp.concatenate(parts, axis=0)


def pick(col, width):
    col = col.astype(I16)
    lane = lax.broadcasted_iota(jnp.int32, col.shape, 1).astype(I16)
    one = jnp.ones(col.shape, BF16)
    zero = jnp.zeros(col.shape, BF16)
    return jnp.concatenate(
        [jnp.where(col == lane + I16(128 * j), one, zero) for j in range(width // 128)], axis=1
    )


def spread(rows, width):
    outs = []
    for i in range(rows.shape[0]):
        ids = jnp.broadcast_to(rows[i : i + 1, :], (128, 128)).astype(I16)
        sub = lax.broadcasted_iota(jnp.int32, (128, 128), 0).astype(I16)
        one = jnp.ones((128, 128), BF16)
        zero = jnp.zeros((128, 128), BF16)
        outs.append(
            jnp.concatenate(
                [jnp.where(ids == sub + I16(128 * j), one, zero) for j in range(width // 128)],
                axis=0,
            )
        )
    return outs[0] if len(outs) == 1 else jnp.concatenate(outs, axis=1)


def halves(value, high):
    zero = jnp.zeros_like(value)
    return jnp.concatenate(
        [jnp.where(high, zero, value), jnp.where(high, value, zero)], axis=1
    ).astype(BF16)


def layer_norm(value):
    center = value - jnp.mean(value, axis=-1, keepdims=True)
    inv = lax.rsqrt(jnp.mean(center * center, axis=-1, keepdims=True) + EPSILON)
    return center * inv, inv


def norm_back(upstream, normed, inv):
    first = jnp.mean(upstream, axis=-1, keepdims=True)
    second = jnp.mean(upstream * normed, axis=-1, keepdims=True)
    return (upstream - first - normed * second) * inv


def silu_pair(pre):
    sig = 0.5 * jnp.tanh(0.5 * pre) + 0.5
    hid = pre * sig
    return hid.astype(BF16), sig + hid * (1.0 - sig)


def whole(n):
    return [pl.BlockSpec(memory_space=pltpu.VMEM)] * n


def anywhere(n):
    return [pl.BlockSpec(memory_space=pl.ANY)] * n


def store_block(total, block, value):
    value = value.astype(BF16)
    for half in range(2):
        for i in range(4):
            for j in range(4):
                total[half, 4 * i + j, 16 * block : 16 * block + 16, :] = value[
                    64 * half + 16 * i : 64 * half + 16 * i + 16, 128 * j : 128 * j + 128
                ]


def load_block(out, block, scale):
    lines = []
    for half in range(2):
        for i in range(4):
            lines.append(
                jnp.concatenate(
                    [out[half, 4 * i + j, 16 * block : 16 * block + 16, :] for j in range(4)],
                    axis=1,
                )
            )
    return jnp.concatenate(lines, axis=0).astype(F32) * scale


def distance(k):
    dx, dy = k // 4, k % 4
    return min(dx, 4 - dx) + min(dy, 4 - dy)


FAR_FIRST = sorted(range(1, NB), key=distance, reverse=True)
BATCHES = [[k for k in range(1, NB) if distance(k) in near] for near in ((1,), (2,), (3, 4))]


def ahead(me, k):
    return lax.rem(me // 4 + k // 4, 4) * 4 + lax.rem(lax.rem(me, 4) + k % 4, 4)


def behind(me, k):
    return lax.rem(me // 4 + 4 - k // 4, 4) * 4 + lax.rem(lax.rem(me, 4) + 4 - k % 4, 4)


def remote(src, dst, send, recv, to):
    return pltpu.make_async_remote_copy(
        src_ref=src, dst_ref=dst, send_sem=send, recv_sem=recv, device_id=to, device_id_type=MESH
    )


class Reduce:
    def __init__(self, me, grp, total, out, half_in, mine, piece_in, own, z_in, sems):
        self.me, self.grp = me, grp
        self.core = lax.rem(grp, 2)
        self.zpos = grp // 2
        self.other = (me, grp + 1 - 2 * self.core)
        self.total, self.out, self.half_in, self.mine = total, out, half_in, mine
        self.piece_in, self.own, self.z_in = piece_in, own, z_in
        self.ps, self.pr, self.ls, self.lr = sems

    def pair(self):
        return remote(
            self.total.at[1 - self.core], self.half_in, self.ps.at[0], self.pr.at[0], self.other
        )

    def piece(self, k):
        to = ahead(self.me, k)
        return remote(
            self.mine.at[to],
            self.piece_in.at[self.me],
            self.ls.at[0, k],
            self.lr.at[0, k],
            (to, self.grp),
        )

    def along_z(self, k):
        to = lax.rem(self.grp + 2 * k, NG)
        return remote(
            self.own, self.z_in.at[self.zpos], self.ps.at[1 + k], self.pr.at[1 + k], (self.me, to)
        )

    def spread(self, k):
        to = ahead(self.me, k)
        place = self.out.at[self.core, self.me]
        return remote(place, place, self.ls.at[1, k], self.lr.at[1, k], (to, self.grp))

    def last(self):
        place = self.out.at[self.core]
        return remote(place, place, self.ps.at[1], self.pr.at[1], self.other)

    def start(self):
        self.pair().start()

    def to_line(self):
        self.pair().wait()
        self.mine[...] = (
            self.total[self.core].astype(F32) + self.half_in[...].astype(F32)
        ).astype(BF16)
        for k in FAR_FIRST:
            self.piece(k).start()
        self.piece_in[self.me] = self.mine[self.me]

    def to_z(self):
        for k in range(1, NB):
            self.piece(k).wait()
        acc = self.piece_in[0].astype(F32)
        for q in range(1, NB):
            acc = acc + self.piece_in[q].astype(F32)
        self.own[...] = acc.astype(BF16)
        for k in range(1, 4):
            self.along_z(k).start()
        self.z_in[self.zpos] = self.own[...]

    def to_all(self):
        for k in range(1, 4):
            self.along_z(k).wait()
        acc = self.z_in[0].astype(F32)
        for q in range(1, 4):
            acc = acc + self.z_in[q].astype(F32)
        self.out[self.core, self.me] = acc.astype(BF16)
        for k in FAR_FIRST:
            self.spread(k).start()

    def to_pair(self):
        for k in range(1, NB):
            self.spread(k).wait()
        self.last().start()

    def end(self):
        self.last().wait()


def main_kernel(
    node_scale,
    wanted_h,
    slot_h,
    receiver_h,
    nodes_h,
    edges_h,
    w_ein_h,
    w_eout_h,
    w_nin_h,
    w_nout_h,
    node_cot_h,
    edge_cot_h,
    new_nodes_h,
    new_edges_h,
    edge_grad_h,
    node_grad_h,
    g_nin_h,
    g_nout_h,
    out_e,
    wanted,
    slot,
    receiver,
    nodes,
    g_acc,
    w_ein,
    w_eout,
    w_nin,
    w_nout,
    node_cot,
    edge_cot,
    asked,
    staged,
    rows_in,
    recv_col,
    send_col,
    pick_recv,
    pick_send,
    spread_recv,
    stacked,
    big,
    hidden,
    slope,
    d_out_all,
    slots2,
    nodes2,
    acc_node,
    acc_slot,
    node_part,
    new_nodes,
    new_edges,
    slot_grad,
    slot_in,
    g_nin,
    g_nout,
    total_n,
    out_n,
    half_n,
    mine_n,
    piece_n,
    own_n,
    z_n,
    total_e,
    half_e,
    mine_e,
    piece_e,
    own_e,
    z_e,
    load_sem,
    store_sem,
    s1,
    r1,
    s2,
    r2,
    s3,
    r3,
    n_ps,
    n_pr,
    n_ls,
    n_lr,
    e_ps,
    e_pr,
    e_ls,
    e_lr,
):
    me = lax.axis_index("blk")
    grp = lax.axis_index("grp")
    barrier = pltpu.get_barrier_semaphore()
    greeted = [(ahead(me, k), grp) for k in FAR_FIRST]
    greeted += [(me, lax.rem(grp + 2 * k, NG)) for k in range(1, 4)]
    greeted += [(me, grp + 1 - 2 * lax.rem(grp, 2))]
    for peer in greeted:
        pl.semaphore_signal(barrier, inc=1, device_id=peer, device_id_type=MESH)

    loads = [
        pltpu.make_async_copy(src, dst, load_sem.at[i])
        for i, (src, dst) in enumerate(
            [
                (nodes_h, nodes),
                (receiver_h, receiver),
                (wanted_h, wanted),
                (slot_h, slot),
                (edges_h, stacked.at[:, pl.ds(0, L)]),
                (w_ein_h, w_ein),
                (w_eout_h, w_eout),
                (w_nin_h, w_nin),
                (w_nout_h, w_nout),
                (node_cot_h, node_cot),
                (edge_cot_h, edge_cot),
            ]
        )
    ]
    for copy in loads:
        copy.start()

    red_n = Reduce(
        me, grp, total_n, out_n, half_n, mine_n, piece_n, own_n, z_n, (n_ps, n_pr, n_ls, n_lr)
    )
    red_e = Reduce(
        me, grp, total_e, out_e, half_e, mine_e, piece_e, own_e, z_e, (e_ps, e_pr, e_ls, e_lr)
    )

    def ask(k):
        to = ahead(me, k)
        return remote(wanted.at[to], asked.at[me], s1.at[k], r1.at[k], (to, grp))

    def give(k):
        to = behind(me, k)
        return remote(staged.at[k], rows_in.at[me], s2.at[k], r2.at[k], (to, grp))

    def give_slot(k):
        to = ahead(me, k)
        return remote(slot_grad.at[to], slot_in.at[me], s3.at[k], r3.at[k], (to, grp))

    loads[0].wait()
    loads[1].wait()
    nodes2[:, :L] = nodes[: GR // 2, :]
    nodes2[:, L:] = nodes[GR // 2 :, :]

    def place(t, size):
        return pl.ds(pl.multiple_of(t * size, size), size)

    def recv_hot(t, carry):
        rows = place(t, TA)
        ids = receiver[pl.ds(t * (TA // 128), TA // 128)].reshape(TA // 128, 128)
        col = column(ids)
        recv_col[rows, :] = col
        hot = pick(col & 511, 512)
        pick_recv[rows, :] = hot
        both = mm(hot, nodes2[...])
        stacked[rows, 2 * L :] = jnp.where(col >= 512, both[:, L:], both[:, :L]).astype(BF16)
        return carry

    loads[2].wait()
    loads[3].wait()
    lax.fori_loop(0, E // TA, recv_hot, 0)

    def send_hot(t, carry):
        rows = place(t, TA)
        ids = slot[pl.ds(t * (TA // 128), TA // 128)].reshape(TA // 128, 128)
        col = column(ids)
        send_col[rows, :] = col
        pick_send[rows, :] = pick(col & 1023, 1024)
        return carry

    lax.fori_loop(0, E // TA, send_hot, 0)
    pl.semaphore_wait(barrier, len(greeted))
    for k in FAR_FIRST:
        ask(k).start()
    asked[me] = wanted[me]

    for copy in loads[4:]:
        copy.wait()

    def part_pre(t, carry):
        rows = place(t, T)
        both = jnp.concatenate([stacked[rows, :L], stacked[rows, 2 * L :]], axis=1)
        weight = jnp.concatenate([w_ein[:L, :], w_ein[2 * L :, :]], axis=0)
        big[rows, :] = mm(both, weight)
        return carry

    lax.fori_loop(0, E // T, part_pre, 0)

    def recv_spread(t, carry):
        ids = receiver[pl.ds(t * (TA // 128), TA // 128)].reshape(TA // 128, 128)
        spread_recv[t] = spread(ids & 511, 512)
        return carry

    lax.fori_loop(0, E // TA, recv_spread, 0)
    def look_up(ids):
        col = column(ids)
        both = mm(pick(col & 511, 512), nodes2[...])
        return jnp.where(col >= 512, both[:, L:], both[:, :L]).astype(BF16)

    rows_in[me] = look_up(asked[me])
    for batch in BATCHES:
        for k in batch:
            ask(k).wait_recv()
        found = look_up(jnp.concatenate([asked[behind(me, k)] for k in batch], axis=0))
        for i, k in enumerate(batch):
            staged[k] = found[128 * i : 128 * i + 128]
        for k in reversed(batch):
            give(k).start()

    acc_node[...] = jnp.zeros_like(acc_node)
    acc_slot[...] = jnp.zeros_like(acc_slot)

    for k in range(1, NB):
        ask(k).wait_send()
        give(k).wait()
    for p in range(8):
        slots2[128 * p : 128 * p + 128, :L] = rows_in[p]
        slots2[128 * p : 128 * p + 128, L:] = rows_in[p + 8]

    def cut(step):
        return slice(step * TA, step * TA + TA)

    def gather(rows):
        both = mm(pick_send[rows, :], slots2[...])
        high = send_col[rows, :] >= 1024
        stacked[rows, L : 2 * L] = jnp.where(high, both[:, L:], both[:, :L]).astype(BF16)

    def first(rows):
        pre = big[rows, :] + mm(stacked[rows, L : 2 * L], w_ein[L : 2 * L, :])
        hid, slp = silu_pair(pre)
        hidden[rows, :] = hid
        slope[rows, :] = slp.astype(BF16)

    def second(rows, t):
        norm, inv = layer_norm(mm(hidden[rows, :], w_eout[...]))
        big[rows, :L] = norm
        big[rows, L : 2 * L] = jnp.broadcast_to(inv, (TA, L))
        message = norm.astype(BF16).astype(F32)
        new_edges[rows, :] = (stacked[rows, :L].astype(F32) + message).astype(BF16)
        acc_node[...] += mm(spread_recv[t], halves(message, recv_col[rows, :] >= 512))

    count = E // TA
    for step in range(count + 2):
        if step < count:
            gather(cut(step))
        if 1 <= step <= count:
            first(cut(step - 1))
        if step >= 2:
            second(cut(step - 2), step - 2)
    stores = [pltpu.make_async_copy(new_edges, new_edges_h, store_sem.at[0])]
    stores[0].start()

    inbound = jnp.concatenate([acc_node[:, :L], acc_node[:, L:]], axis=0).astype(BF16)
    node = nodes[...]
    node_input = jnp.concatenate([node, inbound], axis=1)
    hid, slp = silu_pair(mm(node_input, w_nin[...]))
    norm, inv = layer_norm(mm(hid, w_nout[...]))
    new_nodes[...] = (node.astype(F32) + norm).astype(BF16)
    stores.append(pltpu.make_async_copy(new_nodes, new_nodes_h, store_sem.at[1]))
    stores[1].start()
    cot = node_cot[...].astype(F32)
    d_out = norm_back(cot, norm, inv).astype(BF16)
    d_pre = (mm_nt(d_out, w_nout[...]) * slp).astype(BF16)
    d_in = mm_nt(d_pre, w_nin[...])
    node_part[...] = cot + d_in[:, :L]
    d_inbound = d_in[:, L:].astype(BF16)
    nodes2[:, :L] = d_inbound[: GR // 2, :]
    nodes2[:, L:] = d_inbound[GR // 2 :, :]
    store_block(total_n, 2, mm_tn(d_out, hid))
    g_in = mm_tn(node_input, d_pre)
    store_block(total_n, 0, g_in[:128])
    store_block(total_n, 1, g_in[128:])
    acc_node[...] = jnp.zeros_like(acc_node)
    red_n.start()

    def gather_back(rows):
        both = mm(pick_recv[rows, :], nodes2[...])
        big[rows, 3 * L :] = jnp.where(recv_col[rows, :] >= 512, both[:, L:], both[:, :L])

    def back_norm(rows):
        upstream = edge_cot[rows, :].astype(F32) + big[rows, 3 * L :]
        d_out = norm_back(upstream, big[rows, :L], big[rows, L : 2 * L]).astype(BF16)
        d_out_all[rows, :] = d_out
        slope[rows, :] = (mm_nt(d_out, w_eout[...]) * slope[rows, :].astype(F32)).astype(BF16)

    def weight_grads(rows, t):
        g_in = mm_tn(stacked[rows, :], slope[rows, :])
        g_out = mm_tn(d_out_all[rows, :], hidden[rows, :])
        if t > 0:
            g_in = g_in + g_acc[: 3 * L, :]
            g_out = g_out + g_acc[3 * L :, :]
        if t < count - 1:
            g_acc[: 3 * L, :] = g_in
            g_acc[3 * L :, :] = g_out
        else:
            for b in range(3):
                store_block(total_e, b, g_in[128 * b : 128 * b + 128])
            store_block(total_e, 3, g_out)

    for step in range(count + 2):
        if step < count:
            gather_back(cut(step))
        if 1 <= step <= count:
            back_norm(cut(step - 1))
        if step == 2:
            red_n.to_line()
        if step >= 2:
            weight_grads(cut(step - 2), step - 2)
    red_e.start()

    def back_input(t, carry):
        rows = place(t, TB)
        d_in = mm_nt(slope[rows, :], w_ein[...])
        big[rows, 2 * L : 3 * L] = edge_cot[rows, :].astype(F32) + d_in[:, :L]
        send = slot[pl.ds(t * (TB // 128), TB // 128)].reshape(TB // 128, 128)
        acc_slot[...] += mm(
            spread(send & 1023, 1024), halves(d_in[:, L : 2 * L], send_col[rows, :] >= 1024)
        )
        acc_node[...] += mm(spread_recv[t], halves(d_in[:, 2 * L :], recv_col[rows, :] >= 512))

        @pl.when(t == 0)
        def _():
            red_e.to_line()

        @pl.when(t == 2)
        def _():
            red_n.to_z()

        return carry

    lax.fori_loop(0, E // TB, back_input, 0)
    for p in range(8):
        slot_grad[p] = acc_slot[128 * p : 128 * p + 128, :L].astype(BF16)
        slot_grad[p + 8] = acc_slot[128 * p : 128 * p + 128, L:].astype(BF16)
    for k in FAR_FIRST:
        give_slot(k).start()
    slot_in[me] = slot_grad[me]
    stores.append(
        pltpu.make_async_copy(big.at[:, pl.ds(2 * L, L)], edge_grad_h, store_sem.at[2])
    )
    stores[2].start()
    red_n.to_all()
    red_e.to_z()
    node_part[: GR // 2, :] += acc_node[:, :L]
    node_part[GR // 2 :, :] += acc_node[:, L:]
    red_e.to_all()
    red_n.to_pair()
    red_n.end()
    for b in range(2):
        g_nin[128 * b : 128 * b + 128, :] = load_block(out_n, b, node_scale)
    g_nout[...] = jnp.transpose(load_block(out_n, 2, node_scale))
    stores.append(pltpu.make_async_copy(g_nin, g_nin_h, store_sem.at[3]))
    stores.append(pltpu.make_async_copy(g_nout, g_nout_h, store_sem.at[4]))
    stores[3].start()
    stores[4].start()
    for k in range(1, NB):
        give_slot(k).wait()

    def home(q, carry):
        ids = asked[pl.ds(4 * q, 4)].reshape(4, 128)
        values = slot_in[pl.ds(4 * q, 4)].reshape(4 * 128, L)
        node_part[...] += mm(spread(ids, GR), values)
        return carry

    lax.fori_loop(0, NB // 4, home, 0)
    stores.append(pltpu.make_async_copy(node_part, node_grad_h, store_sem.at[5]))
    stores[5].start()
    red_e.to_pair()
    red_e.end()
    for copy in stores:
        copy.wait()


def main(*args):
    sem = pltpu.SemaphoreType.DMA
    vm = pltpu.VMEM

    def reduce_buffers(blocks, with_out):
        rows = 16 * blocks
        out = [vm((2, NB, rows, L), BF16)] * (2 if with_out else 1)
        return out + [
            vm((NB, rows, L), BF16),
            vm((NB, rows, L), BF16),
            vm((NB, rows, L), BF16),
            vm((rows, L), BF16),
            vm((4, rows, L), BF16),
        ]

    return pl.pallas_call(
        functools.partial(main_kernel, float((GR * NB * NG) ** -0.5)),
        name="message_passing",
        out_shape=(
            jax.ShapeDtypeStruct((GR, L), BF16),
            jax.ShapeDtypeStruct((E, L), BF16),
            jax.ShapeDtypeStruct((E, L), F32),
            jax.ShapeDtypeStruct((GR, L), F32),
            jax.ShapeDtypeStruct((2 * L, H), F32),
            jax.ShapeDtypeStruct((H, L), F32),
            jax.ShapeDtypeStruct((2, NB, 16 * EDGE, L), BF16),
        ),
        in_specs=anywhere(11),
        out_specs=anywhere(6) + whole(1),
        scratch_shapes=[
            vm((NB, 1, 128), jnp.int32),
            vm((E // 128, 1, 128), jnp.int32),
            vm((E // 128, 1, 128), jnp.int32),
            vm((GR, L), BF16),
            vm((4 * L, H), F32),
            vm((3 * L, H), BF16),
            vm((H, L), BF16),
            vm((2 * L, H), BF16),
            vm((H, L), BF16),
            vm((GR, L), BF16),
            vm((E, L), BF16),
            vm((NB, 1, 128), jnp.int32),
            vm((NB, 128, L), BF16),
            vm((NB, 128, L), BF16),
            vm((E, L), jnp.int32),
            vm((E, L), jnp.int32),
            vm((E, 512), BF16),
            vm((E, 1024), BF16),
            vm((E // TA, 512, TA), BF16),
            vm((E, 3 * L), BF16),
            vm((E, H), F32),
            vm((E, H), BF16),
            vm((E, H), BF16),
            vm((E, L), BF16),
            vm((GR, 2 * L), BF16),
            vm((GR // 2, 2 * L), BF16),
            vm((GR // 2, 2 * L), F32),
            vm((GR, 2 * L), F32),
            vm((GR, L), F32),
            vm((GR, L), BF16),
            vm((E, L), BF16),
            vm((NB, 128, L), BF16),
            vm((NB, 128, L), BF16),
            vm((2 * L, H), F32),
            vm((H, L), F32),
        ]
        + reduce_buffers(NODE, True)
        + reduce_buffers(EDGE, False)
        + [sem((11,)), sem((6,))]
        + [sem((NB,))] * 6
        + [sem((5,)), sem((5,)), sem((2, NB)), sem((2, NB))] * 2,
        compiler_params=pltpu.CompilerParams(
            collective_id=0, has_side_effects=True, vmem_limit_bytes=VMEM_LIMIT
        ),
    )(*args)


def finish_kernel(edge_scale, *refs):
    count = 7
    sources, targets = refs[:count], refs[count : 2 * count - 1]
    g_ein_h, g_eout_h = refs[2 * count - 1 : 2 * count + 1]
    held = refs[2 * count + 1 : 3 * count + 1]
    g_ein, g_eout, load_sem, store_sem = refs[3 * count + 1 :]
    loads = [
        pltpu.make_async_copy(sources[i], held[i], load_sem.at[i]) for i in range(count)
    ]
    stores = [
        pltpu.make_async_copy(held[i + 1], targets[i], store_sem.at[i]) for i in range(count - 1)
    ]
    stores += [
        pltpu.make_async_copy(g_ein, g_ein_h, store_sem.at[count - 1]),
        pltpu.make_async_copy(g_eout, g_eout_h, store_sem.at[count]),
    ]
    for copy in loads:
        copy.start()
    out = held[0]
    loads[0].wait()
    for b in range(3):
        g_ein[128 * b : 128 * b + 128, :] = load_block(out, b, edge_scale)
    stores[-2].start()
    g_eout[...] = jnp.transpose(load_block(out, 3, edge_scale))
    stores[-1].start()
    for load, store in zip(loads[1:], stores):
        load.wait()
        store.start()
    for copy in stores:
        copy.wait()


def finish(out, *arrays):
    grads = (
        jax.ShapeDtypeStruct((3 * L, H), F32),
        jax.ShapeDtypeStruct((H, L), F32),
    )
    return pl.pallas_call(
        functools.partial(finish_kernel, float((E * NB * NG) ** -0.5)),
        name="finish",
        out_shape=tuple(jax.ShapeDtypeStruct(a.shape, a.dtype) for a in arrays) + grads,
        in_specs=anywhere(7),
        out_specs=anywhere(8),
        scratch_shapes=[pltpu.VMEM(a.shape, a.dtype) for a in (out,) + arrays + grads]
        + [pltpu.SemaphoreType.DMA((7,)), pltpu.SemaphoreType.DMA((8,))],
        compiler_params=pltpu.CompilerParams(vmem_limit_bytes=VMEM_LIMIT),
    )(out, *arrays)


def on_device(
    nodes,
    edges,
    wanted_rows,
    sender_slot,
    receiver,
    w_edge_in,
    w_edge_out,
    w_node_in,
    w_node_out,
    node_cot,
    edge_cot,
):
    *arrays, out = main(
        wanted_rows.reshape(NB, 1, 128),
        sender_slot.reshape(E // 128, 1, 128),
        receiver.reshape(E // 128, 1, 128),
        nodes,
        edges,
        w_edge_in,
        w_edge_out,
        w_node_in,
        w_node_out,
        node_cot,
        edge_cot,
    )
    new_nodes, new_edges, edge_grad, node_grad, g_nin, g_nout, g_ein, g_eout = finish(out, *arrays)
    return new_nodes, new_edges, node_grad, edge_grad, g_ein, g_eout, g_nin, g_nout


def solution(mesh):
    split = P(("blk", "grp"), None)
    line = P(("blk", "grp"))
    return jax.shard_map(
        on_device,
        mesh=mesh,
        in_specs=(split, split, split, line, line, P(), P(), P(), P(), split, split),
        out_specs=(split, split, split, split, P(), P(), P(), P()),
        check_vma=False,
    )
```

```python
import functools

import jax
import jax.numpy as jnp
from jax import lax
from jax.experimental import pallas as pl
from jax.experimental.pallas import tpu as pltpu
from jax.sharding import PartitionSpec as P

EPSILON = 1e-05
L = 128
H = 512
NB = 16
NG = 8
GR = 1024
E = 4096
T = 2048
TA = 1024
TB = 1024
EDGE = 4
NODE = 3
F32 = jnp.float32
BF16 = jnp.bfloat16
I16 = jnp.int16
VMEM_LIMIT = 63 * 1024 * 1024
MESH = pl.DeviceIdType.MESH


def mm(a, b):
    return jnp.dot(a, b, preferred_element_type=F32)


def mm_nt(a, b):
    return lax.dot_general(a, b, (((1,), (1,)), ((), ())), preferred_element_type=F32)


def mm_tn(a, b):
    return lax.dot_general(a, b, (((0,), (0,)), ((), ())), preferred_element_type=F32)


def column(rows):
    parts = [
        jnp.transpose(jnp.broadcast_to(rows[i : i + 1, :], (128, 128)))
        for i in range(rows.shape[0])
    ]
    return parts[0] if len(parts) == 1 else jnp.concatenate(parts, axis=0)


def pick(col, width):
    col = col.astype(I16)
    lane = lax.broadcasted_iota(jnp.int32, col.shape, 1).astype(I16)
    one = jnp.ones(col.shape, BF16)
    zero = jnp.zeros(col.shape, BF16)
    return jnp.concatenate(
        [jnp.where(col == lane + I16(128 * j), one, zero) for j in range(width // 128)], axis=1
    )


def spread(rows, width):
    outs = []
    for i in range(rows.shape[0]):
        ids = jnp.broadcast_to(rows[i : i + 1, :], (128, 128)).astype(I16)
        sub = lax.broadcasted_iota(jnp.int32, (128, 128), 0).astype(I16)
        one = jnp.ones((128, 128), BF16)
        zero = jnp.zeros((128, 128), BF16)
        outs.append(
            jnp.concatenate(
                [jnp.where(ids == sub + I16(128 * j), one, zero) for j in range(width // 128)],
                axis=0,
            )
        )
    return outs[0] if len(outs) == 1 else jnp.concatenate(outs, axis=1)


def halves(value, high):
    zero = jnp.zeros_like(value)
    return jnp.concatenate(
        [jnp.where(high, zero, value), jnp.where(high, value, zero)], axis=1
    ).astype(BF16)


def layer_norm(value):
    center = value - jnp.mean(value, axis=-1, keepdims=True)
    inv = lax.rsqrt(jnp.mean(center * center, axis=-1, keepdims=True) + EPSILON)
    return center * inv, inv


def norm_back(upstream, normed, inv):
    first = jnp.mean(upstream, axis=-1, keepdims=True)
    second = jnp.mean(upstream * normed, axis=-1, keepdims=True)
    return (upstream - first - normed * second) * inv


def silu_pair(pre):
    sig = 0.5 * jnp.tanh(0.5 * pre) + 0.5
    hid = pre * sig
    return hid.astype(BF16), sig + hid * (1.0 - sig)


def whole(n):
    return [pl.BlockSpec(memory_space=pltpu.VMEM)] * n


def anywhere(n):
    return [pl.BlockSpec(memory_space=pl.ANY)] * n


def store_block(total, block, value):
    value = value.astype(BF16)
    for half in range(2):
        for i in range(4):
            for j in range(4):
                total[half, 4 * i + j, 16 * block : 16 * block + 16, :] = value[
                    64 * half + 16 * i : 64 * half + 16 * i + 16, 128 * j : 128 * j + 128
                ]


def load_block(out, block, scale):
    lines = []
    for half in range(2):
        for i in range(4):
            lines.append(
                jnp.concatenate(
                    [out[half, 4 * i + j, 16 * block : 16 * block + 16, :] for j in range(4)],
                    axis=1,
                )
            )
    return jnp.concatenate(lines, axis=0).astype(F32) * scale


def distance(k):
    dx, dy = k // 4, k % 4
    return min(dx, 4 - dx) + min(dy, 4 - dy)


FAR_FIRST = sorted(range(1, NB), key=distance, reverse=True)
BATCHES = [[k for k in range(1, NB) if distance(k) in near] for near in ((1,), (2,), (3, 4))]


def ahead(me, k):
    return lax.rem(me // 4 + k // 4, 4) * 4 + lax.rem(lax.rem(me, 4) + k % 4, 4)


def behind(me, k):
    return lax.rem(me // 4 + 4 - k // 4, 4) * 4 + lax.rem(lax.rem(me, 4) + 4 - k % 4, 4)


def remote(src, dst, send, recv, to):
    return pltpu.make_async_remote_copy(
        src_ref=src, dst_ref=dst, send_sem=send, recv_sem=recv, device_id=to, device_id_type=MESH
    )


class Reduce:
    def __init__(self, me, grp, total, out, target, half_in, mine, piece_in, own, z_in, sems):
        self.me, self.grp = me, grp
        self.core = lax.rem(grp, 2)
        self.zpos = grp // 2
        self.other = (me, grp + 1 - 2 * self.core)
        self.total, self.out, self.target = total, out, target
        self.half_in, self.mine = half_in, mine
        self.piece_in, self.own, self.z_in = piece_in, own, z_in
        self.ps, self.pr, self.ls, self.lr = sems

    def pair(self):
        return remote(
            self.total.at[1 - self.core], self.half_in, self.ps.at[0], self.pr.at[0], self.other
        )

    def piece(self, k):
        to = ahead(self.me, k)
        return remote(
            self.mine.at[to],
            self.piece_in.at[self.me],
            self.ls.at[0, k],
            self.lr.at[0, k],
            (to, self.grp),
        )

    def along_z(self, k):
        to = lax.rem(self.grp + 2 * k, NG)
        return remote(
            self.own, self.z_in.at[self.zpos], self.ps.at[1 + k], self.pr.at[1 + k], (self.me, to)
        )

    def spread(self, k):
        to = ahead(self.me, k)
        place = self.out.at[self.core, self.me]
        return remote(place, place, self.ls.at[1, k], self.lr.at[1, k], (to, self.grp))

    def last(self):
        return remote(
            self.out.at[self.core],
            self.target.at[self.core],
            self.ps.at[1],
            self.pr.at[1],
            self.other,
        )

    def start(self):
        self.pair().start()

    def to_line(self):
        self.pair().wait()
        self.mine[...] = (
            self.total[self.core].astype(F32) + self.half_in[...].astype(F32)
        ).astype(BF16)
        for k in FAR_FIRST:
            self.piece(k).start()
        self.piece_in[self.me] = self.mine[self.me]

    def to_z(self):
        for k in range(1, NB):
            self.piece(k).wait()
        acc = self.piece_in[0].astype(F32)
        for q in range(1, NB):
            acc = acc + self.piece_in[q].astype(F32)
        self.own[...] = acc.astype(BF16)
        for k in range(1, 4):
            self.along_z(k).start()
        self.z_in[self.zpos] = self.own[...]

    def to_all(self):
        for k in range(1, 4):
            self.along_z(k).wait()
        acc = self.z_in[0].astype(F32)
        for q in range(1, 4):
            acc = acc + self.z_in[q].astype(F32)
        self.out[self.core, self.me] = acc.astype(BF16)
        for k in FAR_FIRST:
            self.spread(k).start()

    def to_pair(self):
        for k in range(1, NB):
            self.spread(k).wait()
        self.last().start()

    def end(self):
        self.last().wait()


def main_kernel(
    node_scale,
    wanted_h,
    slot_h,
    receiver_h,
    nodes_h,
    edges_h,
    w_ein_h,
    w_eout_h,
    w_nin_h,
    w_nout_h,
    node_cot_h,
    edge_cot_h,
    new_nodes_h,
    new_edges_h,
    edge_grad_h,
    node_grad_h,
    g_nin_h,
    g_nout_h,
    out_h,
    wanted,
    slot,
    receiver,
    nodes,
    w_ein,
    w_eout,
    w_nin,
    w_nout,
    node_cot,
    edge_cot,
    asked,
    staged,
    rows_in,
    recv_col,
    send_col,
    pick_recv,
    pick_send,
    spread_recv,
    stacked,
    big,
    hidden,
    slope,
    d_out_all,
    slots2,
    nodes2,
    acc_node,
    acc_slot,
    node_part,
    new_nodes,
    new_edges,
    slot_grad,
    slot_in,
    g_nin,
    g_nout,
    total_n,
    out_n,
    half_n,
    mine_n,
    piece_n,
    own_n,
    z_n,
    total_e,
    out_e,
    half_e,
    mine_e,
    piece_e,
    own_e,
    z_e,
    load_sem,
    store_sem,
    s1,
    r1,
    s2,
    r2,
    s3,
    r3,
    n_ps,
    n_pr,
    n_ls,
    n_lr,
    e_ps,
    e_pr,
    e_ls,
    e_lr,
):
    me = lax.axis_index("blk")
    grp = lax.axis_index("grp")
    barrier = pltpu.get_barrier_semaphore()
    greeted = [(ahead(me, k), grp) for k in FAR_FIRST]
    greeted += [(me, lax.rem(grp + 2 * k, NG)) for k in range(1, 4)]
    greeted += [(me, grp + 1 - 2 * lax.rem(grp, 2))]
    for peer in greeted:
        pl.semaphore_signal(barrier, inc=1, device_id=peer, device_id_type=MESH)

    loads = [
        pltpu.make_async_copy(src, dst, load_sem.at[i])
        for i, (src, dst) in enumerate(
            [
                (nodes_h, nodes),
                (receiver_h, receiver),
                (wanted_h, wanted),
                (slot_h, slot),
                (edges_h, stacked.at[:, pl.ds(0, L)]),
                (w_ein_h, w_ein),
                (w_eout_h, w_eout),
                (w_nin_h, w_nin),
                (w_nout_h, w_nout),
                (node_cot_h, node_cot),
                (edge_cot_h, edge_cot),
            ]
        )
    ]
    for copy in loads:
        copy.start()

    red_n = Reduce(
        me,
        grp,
        total_n,
        out_n,
        out_n,
        half_n,
        mine_n,
        piece_n,
        own_n,
        z_n,
        (n_ps, n_pr, n_ls, n_lr),
    )
    red_e = Reduce(
        me,
        grp,
        total_e,
        out_e,
        out_h,
        half_e,
        mine_e,
        piece_e,
        own_e,
        z_e,
        (e_ps, e_pr, e_ls, e_lr),
    )

    def ask(k):
        to = ahead(me, k)
        return remote(wanted.at[to], asked.at[me], s1.at[k], r1.at[k], (to, grp))

    def give(k):
        to = behind(me, k)
        return remote(staged.at[k], rows_in.at[me], s2.at[k], r2.at[k], (to, grp))

    def give_slot(k):
        to = ahead(me, k)
        return remote(slot_grad.at[to], slot_in.at[me], s3.at[k], r3.at[k], (to, grp))

    loads[0].wait()
    loads[1].wait()
    nodes2[:, :L] = nodes[: GR // 2, :]
    nodes2[:, L:] = nodes[GR // 2 :, :]

    def place(t, size):
        return pl.ds(pl.multiple_of(t * size, size), size)

    def recv_hot(t, carry):
        rows = place(t, TA)
        ids = receiver[pl.ds(t * (TA // 128), TA // 128)].reshape(TA // 128, 128)
        col = column(ids)
        recv_col[rows, :] = col.astype(I16)
        hot = pick(col & 511, 512)
        pick_recv[rows, :] = hot
        both = mm(hot, nodes2[...])
        stacked[rows, 2 * L :] = jnp.where(col >= 512, both[:, L:], both[:, :L]).astype(BF16)
        return carry

    loads[2].wait()
    loads[3].wait()
    lax.fori_loop(0, E // TA, recv_hot, 0)

    def send_hot(t, carry):
        rows = place(t, TA)
        ids = slot[pl.ds(t * (TA // 128), TA // 128)].reshape(TA // 128, 128)
        col = column(ids)
        send_col[rows, :] = col.astype(I16)
        pick_send[rows, :] = pick(col & 1023, 1024)
        return carry

    lax.fori_loop(0, E // TA, send_hot, 0)
    pl.semaphore_wait(barrier, len(greeted))
    for k in FAR_FIRST:
        ask(k).start()
    asked[me] = wanted[me]

    for copy in loads[4:]:
        copy.wait()

    def part_pre(t, carry):
        rows = place(t, T)
        both = jnp.concatenate([stacked[rows, :L], stacked[rows, 2 * L :]], axis=1)
        weight = jnp.concatenate([w_ein[:L, :], w_ein[2 * L :, :]], axis=0)
        big[rows, :] = mm(both, weight)
        return carry

    lax.fori_loop(0, E // T, part_pre, 0)

    def recv_spread(t, carry):
        ids = receiver[pl.ds(t * (TA // 128), TA // 128)].reshape(TA // 128, 128)
        spread_recv[t] = spread(ids & 511, 512)
        return carry

    lax.fori_loop(0, E // TA, recv_spread, 0)
    def look_up(ids):
        col = column(ids)
        both = mm(pick(col & 511, 512), nodes2[...])
        return jnp.where(col >= 512, both[:, L:], both[:, :L]).astype(BF16)

    rows_in[me] = look_up(asked[me])
    for batch in BATCHES:
        for k in batch:
            ask(k).wait_recv()
        found = look_up(jnp.concatenate([asked[behind(me, k)] for k in batch], axis=0))
        for i, k in enumerate(batch):
            staged[k] = found[128 * i : 128 * i + 128]
        for k in reversed(batch):
            give(k).start()


    for k in range(1, NB):
        ask(k).wait_send()
        give(k).wait()
    for p in range(8):
        slots2[128 * p : 128 * p + 128, :L] = rows_in[p]
        slots2[128 * p : 128 * p + 128, L:] = rows_in[p + 8]

    def cut(step):
        return slice(step * TA, step * TA + TA)

    def gather(rows):
        both = mm(pick_send[rows, :], slots2[...])
        high = send_col[rows, :].astype(jnp.int32) >= 1024
        stacked[rows, L : 2 * L] = jnp.where(high, both[:, L:], both[:, :L]).astype(BF16)

    def first(rows):
        pre = big[rows, :] + mm(stacked[rows, L : 2 * L], w_ein[L : 2 * L, :])
        hid, slp = silu_pair(pre)
        hidden[rows, :] = hid
        slope[rows, :] = slp.astype(BF16)

    def second(rows, t):
        norm, inv = layer_norm(mm(hidden[rows, :], w_eout[...]))
        big[rows, :L] = norm
        big[rows, L : 2 * L] = jnp.broadcast_to(inv, (TA, L))
        message = norm.astype(BF16).astype(F32)
        new_edges[rows, :] = (stacked[rows, :L].astype(F32) + message).astype(BF16)
        to_node = mm(spread_recv[t], halves(message, recv_col[rows, :].astype(jnp.int32) >= 512))
        acc_node[...] = to_node if t == 0 else acc_node[...] + to_node

    count = E // TA
    for step in range(count + 2):
        if step < count:
            gather(cut(step))
        if 1 <= step <= count:
            first(cut(step - 1))
        if step >= 2:
            second(cut(step - 2), step - 2)
    stores = [pltpu.make_async_copy(new_edges, new_edges_h, store_sem.at[0])]
    stores[0].start()

    inbound = jnp.concatenate([acc_node[:, :L], acc_node[:, L:]], axis=0).astype(BF16)
    node = nodes[...]
    node_input = jnp.concatenate([node, inbound], axis=1)
    hid, slp = silu_pair(mm(node_input, w_nin[...]))
    norm, inv = layer_norm(mm(hid, w_nout[...]))
    new_nodes[...] = (node.astype(F32) + norm).astype(BF16)
    stores.append(pltpu.make_async_copy(new_nodes, new_nodes_h, store_sem.at[1]))
    stores[1].start()
    cot = node_cot[...].astype(F32)
    d_out = norm_back(cot, norm, inv).astype(BF16)
    d_pre = (mm_nt(d_out, w_nout[...]) * slp).astype(BF16)
    d_in = mm_nt(d_pre, w_nin[...])
    d_inbound = d_in[:, L:].astype(BF16)
    nodes2[:, :L] = d_inbound[: GR // 2, :]
    nodes2[:, L:] = d_inbound[GR // 2 :, :]

    def node_grads():
        node_part[...] = cot + d_in[:, :L]
        store_block(total_n, 2, mm_tn(d_out, hid))
        g_in = mm_tn(node_input, d_pre)
        store_block(total_n, 0, g_in[:128])
        store_block(total_n, 1, g_in[128:])


    def gather_back(rows):
        both = mm(pick_recv[rows, :], nodes2[...])
        big[rows, 3 * L :] = jnp.where(recv_col[rows, :].astype(jnp.int32) >= 512, both[:, L:], both[:, :L])

    def back_norm(rows):
        upstream = edge_cot[rows, :].astype(F32) + big[rows, 3 * L :]
        d_out = norm_back(upstream, big[rows, :L], big[rows, L : 2 * L]).astype(BF16)
        d_out_all[rows, :] = d_out
        slope[rows, :] = (mm_nt(d_out, w_eout[...]) * slope[rows, :].astype(F32)).astype(BF16)

    def weight_grads(rows, t):
        g_in = mm_tn(stacked[rows, :], slope[rows, :])
        g_out = mm_tn(d_out_all[rows, :], hidden[rows, :])
        if t > 0:
            g_in = g_in + jnp.concatenate([acc_slot[:384, :], acc_slot[384:768, :]], axis=1)
            g_out = g_out + jnp.concatenate([acc_slot[768:896, :], acc_slot[896:, :]], axis=1)
        if t < count - 1:
            acc_slot[:384, :] = g_in[:, : H // 2]
            acc_slot[384:768, :] = g_in[:, H // 2 :]
            acc_slot[768:896, :] = g_out[:, : H // 2]
            acc_slot[896:, :] = g_out[:, H // 2 :]
        else:
            for b in range(3):
                store_block(total_e, b, g_in[128 * b : 128 * b + 128])
            store_block(total_e, 3, g_out)

    for step in range(count + 2):
        if step < count:
            gather_back(cut(step))
        if step == 0:
            node_grads()
            red_n.start()
        if 1 <= step <= count:
            back_norm(cut(step - 1))
        if step == 2:
            red_n.to_line()
        if step >= 2:
            weight_grads(cut(step - 2), step - 2)
    red_e.start()

    def back_input(rows):
        d_in = mm_nt(slope[rows, :], w_ein[...])
        big[rows, 2 * L : 3 * L] = edge_cot[rows, :].astype(F32) + d_in[:, :L]
        pick_send[rows, : 2 * L] = halves(d_in[:, L : 2 * L], send_col[rows, :].astype(jnp.int32) >= 1024)
        pick_send[rows, 2 * L : 4 * L] = halves(d_in[:, 2 * L :], recv_col[rows, :].astype(jnp.int32) >= 512)

    def scatter(rows, t):
        send = slot[TA // 128 * t : TA // 128 * (t + 1)].reshape(TA // 128, 128)
        to_slot = mm(spread(send & 1023, 1024), pick_send[rows, : 2 * L])
        to_node = mm(spread_recv[t], pick_send[rows, 2 * L : 4 * L])
        acc_slot[...] = to_slot if t == 0 else acc_slot[...] + to_slot
        acc_node[...] = to_node if t == 0 else acc_node[...] + to_node

    for step in range(count + 1):
        if step < count:
            back_input(cut(step))
        if step == 0:
            red_e.to_line()
        if step >= 1:
            scatter(cut(step - 1), step - 1)
    for p in range(8):
        slot_grad[p] = acc_slot[128 * p : 128 * p + 128, :L].astype(BF16)
        slot_grad[p + 8] = acc_slot[128 * p : 128 * p + 128, L:].astype(BF16)
    for k in FAR_FIRST:
        give_slot(k).start()
    slot_in[me] = slot_grad[me]
    stores.append(
        pltpu.make_async_copy(big.at[:, pl.ds(2 * L, L)], edge_grad_h, store_sem.at[2])
    )
    stores[2].start()
    node_part[: GR // 2, :] += acc_node[:, :L]
    node_part[GR // 2 :, :] += acc_node[:, L:]
    red_n.to_z()
    red_e.to_z()
    red_n.to_all()
    red_e.to_all()
    for k in range(1, NB):
        give_slot(k).wait()

    def home(q, carry):
        ids = asked[pl.ds(4 * q, 4)].reshape(4, 128)
        values = slot_in[pl.ds(4 * q, 4)].reshape(4 * 128, L)
        node_part[...] += mm(spread(ids, GR), values)
        return carry

    lax.fori_loop(0, NB // 4, home, 0)
    stores.append(pltpu.make_async_copy(node_part, node_grad_h, store_sem.at[5]))
    stores[3].start()
    red_n.to_pair()
    red_n.end()
    for b in range(2):
        g_nin[128 * b : 128 * b + 128, :] = load_block(out_n, b, node_scale)
    g_nout[...] = jnp.transpose(load_block(out_n, 2, node_scale))
    stores.append(pltpu.make_async_copy(g_nin, g_nin_h, store_sem.at[3]))
    stores.append(pltpu.make_async_copy(g_nout, g_nout_h, store_sem.at[4]))
    stores[4].start()
    stores[5].start()
    red_e.to_pair()
    core = lax.rem(grp, 2)
    stores.append(pltpu.make_async_copy(out_e.at[core], out_h.at[core], store_sem.at[6]))
    stores[6].start()
    red_e.end()
    for copy in stores:
        copy.wait()


def main(*args):
    sem = pltpu.SemaphoreType.DMA
    vm = pltpu.VMEM

    def reduce_buffers(blocks):
        rows = 16 * blocks
        return [vm((2, NB, rows, L), BF16)] * 2 + [
            vm((NB, rows, L), BF16),
            vm((NB, rows, L), BF16),
            vm((NB, rows, L), BF16),
            vm((rows, L), BF16),
            vm((4, rows, L), BF16),
        ]

    return pl.pallas_call(
        functools.partial(main_kernel, float((GR * NB * NG) ** -0.5)),
        name="message_passing",
        out_shape=(
            jax.ShapeDtypeStruct((GR, L), BF16),
            jax.ShapeDtypeStruct((E, L), BF16),
            jax.ShapeDtypeStruct((E, L), F32),
            jax.ShapeDtypeStruct((GR, L), F32),
            jax.ShapeDtypeStruct((2 * L, H), F32),
            jax.ShapeDtypeStruct((H, L), F32),
            jax.ShapeDtypeStruct((2, NB, 16 * EDGE, L), BF16),
        ),
        in_specs=anywhere(11),
        out_specs=anywhere(7),
        scratch_shapes=[
            vm((NB, 1, 128), jnp.int32),
            vm((E // 128, 1, 128), jnp.int32),
            vm((E // 128, 1, 128), jnp.int32),
            vm((GR, L), BF16),
            vm((3 * L, H), BF16),
            vm((H, L), BF16),
            vm((2 * L, H), BF16),
            vm((H, L), BF16),
            vm((GR, L), BF16),
            vm((E, L), BF16),
            vm((NB, 1, 128), jnp.int32),
            vm((NB, 128, L), BF16),
            vm((NB, 128, L), BF16),
            vm((E, L), I16),
            vm((E, L), I16),
            vm((E, 512), BF16),
            vm((E, 1024), BF16),
            vm((E // TA, 512, TA), BF16),
            vm((E, 3 * L), BF16),
            vm((E, H), F32),
            vm((E, H), BF16),
            vm((E, H), BF16),
            vm((E, L), BF16),
            vm((GR, 2 * L), BF16),
            vm((GR // 2, 2 * L), BF16),
            vm((GR // 2, 2 * L), F32),
            vm((GR, 2 * L), F32),
            vm((GR, L), F32),
            vm((GR, L), BF16),
            vm((E, L), BF16),
            vm((NB, 128, L), BF16),
            vm((NB, 128, L), BF16),
            vm((2 * L, H), F32),
            vm((H, L), F32),
        ]
        + reduce_buffers(NODE)
        + reduce_buffers(EDGE)
        + [sem((11,)), sem((7,))]
        + [sem((NB,))] * 6
        + [sem((5,)), sem((5,)), sem((2, NB)), sem((2, NB))] * 2,
        compiler_params=pltpu.CompilerParams(
            collective_id=0, has_side_effects=True, vmem_limit_bytes=VMEM_LIMIT
        ),
    )(*args)


def finish_kernel(edge_scale, *refs):
    count = 7
    sources, targets = refs[:count], refs[count : 2 * count - 1]
    g_ein_h, g_eout_h = refs[2 * count - 1 : 2 * count + 1]
    held = refs[2 * count + 1 : 3 * count + 1]
    g_ein, g_eout, load_sem, store_sem = refs[3 * count + 1 :]
    loads = [
        pltpu.make_async_copy(sources[i], held[i], load_sem.at[i]) for i in range(count)
    ]
    stores = [
        pltpu.make_async_copy(held[i + 1], targets[i], store_sem.at[i]) for i in range(count - 1)
    ]
    stores += [
        pltpu.make_async_copy(g_ein, g_ein_h, store_sem.at[count - 1]),
        pltpu.make_async_copy(g_eout, g_eout_h, store_sem.at[count]),
    ]
    for copy in loads:
        copy.start()
    out = held[0]
    loads[0].wait()
    for b in range(3):
        g_ein[128 * b : 128 * b + 128, :] = load_block(out, b, edge_scale)
    stores[-2].start()
    g_eout[...] = jnp.transpose(load_block(out, 3, edge_scale))
    stores[-1].start()
    for load, store in zip(loads[1:], stores):
        load.wait()
        store.start()
    for copy in stores:
        copy.wait()


def finish(out, *arrays):
    grads = (
        jax.ShapeDtypeStruct((3 * L, H), F32),
        jax.ShapeDtypeStruct((H, L), F32),
    )
    return pl.pallas_call(
        functools.partial(finish_kernel, float((E * NB * NG) ** -0.5)),
        name="finish",
        out_shape=tuple(jax.ShapeDtypeStruct(a.shape, a.dtype) for a in arrays) + grads,
        in_specs=anywhere(7),
        out_specs=anywhere(8),
        scratch_shapes=[pltpu.VMEM(a.shape, a.dtype) for a in (out,) + arrays + grads]
        + [pltpu.SemaphoreType.DMA((7,)), pltpu.SemaphoreType.DMA((8,))],
        compiler_params=pltpu.CompilerParams(vmem_limit_bytes=VMEM_LIMIT),
    )(out, *arrays)


def on_device(
    nodes,
    edges,
    wanted_rows,
    sender_slot,
    receiver,
    w_edge_in,
    w_edge_out,
    w_node_in,
    w_node_out,
    node_cot,
    edge_cot,
):
    *arrays, out = main(
        wanted_rows.reshape(NB, 1, 128),
        sender_slot.reshape(E // 128, 1, 128),
        receiver.reshape(E // 128, 1, 128),
        nodes,
        edges,
        w_edge_in,
        w_edge_out,
        w_node_in,
        w_node_out,
        node_cot,
        edge_cot,
    )
    new_nodes, new_edges, edge_grad, node_grad, g_nin, g_nout, g_ein, g_eout = finish(out, *arrays)
    return new_nodes, new_edges, node_grad, edge_grad, g_ein, g_eout, g_nin, g_nout


def solution(mesh):
    split = P(("blk", "grp"), None)
    line = P(("blk", "grp"))
    return jax.shard_map(
        on_device,
        mesh=mesh,
        in_specs=(split, split, split, line, line, P(), P(), P(), P(), split, split),
        out_specs=(split, split, split, split, P(), P(), P(), P()),
        check_vma=False,
    )
```

```python
import functools

import jax
import jax.numpy as jnp
from jax import lax
from jax.experimental import pallas as pl
from jax.experimental.pallas import tpu as pltpu
from jax.sharding import PartitionSpec as P

EPSILON = 1e-05
L = 128
H = 512
NB = 16
NG = 8
GR = 1024
E = 4096
T = 2048
TA = 1024
TB = 1024
EDGE = 4
NODE = 3
F32 = jnp.float32
BF16 = jnp.bfloat16
I16 = jnp.int16
VMEM_LIMIT = 63 * 1024 * 1024
MESH = pl.DeviceIdType.MESH


def mm(a, b):
    return jnp.dot(a, b, preferred_element_type=F32)


def mm_nt(a, b):
    return lax.dot_general(a, b, (((1,), (1,)), ((), ())), preferred_element_type=F32)


def mm_tn(a, b):
    return lax.dot_general(a, b, (((0,), (0,)), ((), ())), preferred_element_type=F32)


def column(rows):
    parts = [
        jnp.transpose(jnp.broadcast_to(rows[i : i + 1, :], (128, 128)))
        for i in range(rows.shape[0])
    ]
    return parts[0] if len(parts) == 1 else jnp.concatenate(parts, axis=0)


def pick(col, width):
    col = col.astype(I16)
    lane = lax.broadcasted_iota(jnp.int32, col.shape, 1).astype(I16)
    one = jnp.ones(col.shape, BF16)
    zero = jnp.zeros(col.shape, BF16)
    return jnp.concatenate(
        [jnp.where(col == lane + I16(128 * j), one, zero) for j in range(width // 128)], axis=1
    )


def spread(rows, width):
    outs = []
    for i in range(rows.shape[0]):
        ids = jnp.broadcast_to(rows[i : i + 1, :], (128, 128)).astype(I16)
        sub = lax.broadcasted_iota(jnp.int32, (128, 128), 0).astype(I16)
        one = jnp.ones((128, 128), BF16)
        zero = jnp.zeros((128, 128), BF16)
        outs.append(
            jnp.concatenate(
                [jnp.where(ids == sub + I16(128 * j), one, zero) for j in range(width // 128)],
                axis=0,
            )
        )
    return outs[0] if len(outs) == 1 else jnp.concatenate(outs, axis=1)


def halves(value, high):
    zero = jnp.zeros_like(value)
    return jnp.concatenate(
        [jnp.where(high, zero, value), jnp.where(high, value, zero)], axis=1
    ).astype(BF16)


def layer_norm(value):
    center = value - jnp.mean(value, axis=-1, keepdims=True)
    inv = lax.rsqrt(jnp.mean(center * center, axis=-1, keepdims=True) + EPSILON)
    return center * inv, inv


def norm_back(upstream, normed, inv):
    first = jnp.mean(upstream, axis=-1, keepdims=True)
    second = jnp.mean(upstream * normed, axis=-1, keepdims=True)
    return (upstream - first - normed * second) * inv


def silu_pair(pre):
    sig = 0.5 * jnp.tanh(0.5 * pre) + 0.5
    hid = pre * sig
    return hid.astype(BF16), sig + hid * (1.0 - sig)


def whole(n):
    return [pl.BlockSpec(memory_space=pltpu.VMEM)] * n


def anywhere(n):
    return [pl.BlockSpec(memory_space=pl.ANY)] * n


def store_block(total, block, value):
    value = value.astype(BF16)
    for half in range(2):
        for i in range(4):
            for j in range(4):
                total[half, 4 * i + j, 16 * block : 16 * block + 16, :] = value[
                    64 * half + 16 * i : 64 * half + 16 * i + 16, 128 * j : 128 * j + 128
                ]


def load_block(out, block, scale):
    lines = []
    for half in range(2):
        for i in range(4):
            lines.append(
                jnp.concatenate(
                    [out[half, 4 * i + j, 16 * block : 16 * block + 16, :] for j in range(4)],
                    axis=1,
                )
            )
    return jnp.concatenate(lines, axis=0).astype(F32) * scale


def distance(k):
    dx, dy = k // 4, k % 4
    return min(dx, 4 - dx) + min(dy, 4 - dy)


FAR_FIRST = sorted(range(1, NB), key=distance, reverse=True)
BATCHES = [[k for k in range(1, NB) if distance(k) in near] for near in ((1,), (2,), (3, 4))]


def ahead(me, k):
    return lax.rem(me // 4 + k // 4, 4) * 4 + lax.rem(lax.rem(me, 4) + k % 4, 4)


def behind(me, k):
    return lax.rem(me // 4 + 4 - k // 4, 4) * 4 + lax.rem(lax.rem(me, 4) + 4 - k % 4, 4)


def remote(src, dst, send, recv, to):
    return pltpu.make_async_remote_copy(
        src_ref=src, dst_ref=dst, send_sem=send, recv_sem=recv, device_id=to, device_id_type=MESH
    )


class Reduce:
    def __init__(self, me, grp, total, out, target, half_in, mine, piece_in, own, z_in, sems):
        self.me, self.grp = me, grp
        self.core = lax.rem(grp, 2)
        self.zpos = grp // 2
        self.other = (me, grp + 1 - 2 * self.core)
        self.total, self.out, self.target = total, out, target
        self.half_in, self.mine = half_in, mine
        self.piece_in, self.own, self.z_in = piece_in, own, z_in
        self.ps, self.pr, self.ls, self.lr = sems

    def pair(self):
        return remote(
            self.total.at[1 - self.core], self.half_in, self.ps.at[0], self.pr.at[0], self.other
        )

    def piece(self, k):
        to = ahead(self.me, k)
        return remote(
            self.mine.at[to],
            self.piece_in.at[self.me],
            self.ls.at[0, k],
            self.lr.at[0, k],
            (to, self.grp),
        )

    def along_z(self, k):
        to = lax.rem(self.grp + 2 * k, NG)
        return remote(
            self.own, self.z_in.at[self.zpos], self.ps.at[1 + k], self.pr.at[1 + k], (self.me, to)
        )

    def spread(self, k):
        to = ahead(self.me, k)
        place = self.out.at[self.core, self.me]
        return remote(place, place, self.ls.at[1, k], self.lr.at[1, k], (to, self.grp))

    def last(self):
        return remote(
            self.out.at[self.core],
            self.target.at[self.core],
            self.ps.at[1],
            self.pr.at[1],
            self.other,
        )

    def start(self):
        self.pair().start()

    def to_line(self):
        self.pair().wait()
        self.mine[...] = (
            self.total[self.core].astype(F32) + self.half_in[...].astype(F32)
        ).astype(BF16)
        for k in FAR_FIRST:
            self.piece(k).start()
        self.piece_in[self.me] = self.mine[self.me]

    def to_z(self):
        for k in range(1, NB):
            self.piece(k).wait()
        acc = self.piece_in[0].astype(F32)
        for q in range(1, NB):
            acc = acc + self.piece_in[q].astype(F32)
        self.own[...] = acc.astype(BF16)
        for k in range(1, 4):
            self.along_z(k).start()
        self.z_in[self.zpos] = self.own[...]

    def to_all(self):
        for k in range(1, 4):
            self.along_z(k).wait()
        acc = self.z_in[0].astype(F32)
        for q in range(1, 4):
            acc = acc + self.z_in[q].astype(F32)
        self.out[self.core, self.me] = acc.astype(BF16)
        for k in FAR_FIRST:
            self.spread(k).start()

    def to_pair(self):
        for k in range(1, NB):
            self.spread(k).wait()
        self.last().start()

    def end(self):
        self.last().wait()


def main_kernel(
    wanted_h,
    slot_h,
    receiver_h,
    nodes_h,
    edges_h,
    w_ein_h,
    w_eout_h,
    w_nin_h,
    w_nout_h,
    node_cot_h,
    edge_cot_h,
    new_nodes_h,
    new_edges_h,
    edge_grad_h,
    node_grad_h,
    out_nh,
    out_h,
    wanted,
    slot,
    receiver,
    nodes,
    w_ein,
    w_eout,
    w_nin,
    w_nout,
    node_cot,
    edge_cot,
    asked,
    staged,
    rows_in,
    recv_col,
    send_col,
    pick_recv,
    pick_send,
    spread_recv,
    stacked,
    big,
    hidden,
    slope,
    d_out_all,
    slots2,
    nodes2,
    acc_node,
    acc_slot,
    node_part,
    new_nodes,
    new_edges,
    slot_grad,
    slot_in,
    total_n,
    out_n,
    half_n,
    mine_n,
    piece_n,
    own_n,
    z_n,
    total_e,
    out_e,
    half_e,
    mine_e,
    piece_e,
    own_e,
    z_e,
    load_sem,
    store_sem,
    s1,
    r1,
    s2,
    r2,
    s3,
    r3,
    n_ps,
    n_pr,
    n_ls,
    n_lr,
    e_ps,
    e_pr,
    e_ls,
    e_lr,
):
    me = lax.axis_index("blk")
    grp = lax.axis_index("grp")
    barrier = pltpu.get_barrier_semaphore()
    greeted = [(ahead(me, k), grp) for k in FAR_FIRST]
    greeted += [(me, lax.rem(grp + 2 * k, NG)) for k in range(1, 4)]
    greeted += [(me, grp + 1 - 2 * lax.rem(grp, 2))]
    for peer in greeted:
        pl.semaphore_signal(barrier, inc=1, device_id=peer, device_id_type=MESH)

    loads = [
        pltpu.make_async_copy(src, dst, load_sem.at[i])
        for i, (src, dst) in enumerate(
            [
                (nodes_h, nodes),
                (receiver_h, receiver),
                (wanted_h, wanted),
                (slot_h, slot),
                (edges_h, stacked.at[:, pl.ds(0, L)]),
                (w_ein_h, w_ein),
                (w_eout_h, w_eout),
                (w_nin_h, w_nin),
                (w_nout_h, w_nout),
                (node_cot_h, node_cot),
                (edge_cot_h, edge_cot),
            ]
        )
    ]
    for copy in loads:
        copy.start()

    red_n = Reduce(
        me,
        grp,
        total_n,
        out_n,
        out_nh,
        half_n,
        mine_n,
        piece_n,
        own_n,
        z_n,
        (n_ps, n_pr, n_ls, n_lr),
    )
    red_e = Reduce(
        me,
        grp,
        total_e,
        out_e,
        out_h,
        half_e,
        mine_e,
        piece_e,
        own_e,
        z_e,
        (e_ps, e_pr, e_ls, e_lr),
    )

    def ask(k):
        to = ahead(me, k)
        return remote(wanted.at[to], asked.at[me], s1.at[k], r1.at[k], (to, grp))

    def give(k):
        to = behind(me, k)
        return remote(staged.at[k], rows_in.at[me], s2.at[k], r2.at[k], (to, grp))

    def give_slot(k):
        to = ahead(me, k)
        return remote(slot_grad.at[to], slot_in.at[me], s3.at[k], r3.at[k], (to, grp))

    loads[0].wait()
    loads[1].wait()
    nodes2[:, :L] = nodes[: GR // 2, :]
    nodes2[:, L:] = nodes[GR // 2 :, :]

    def place(t, size):
        return pl.ds(pl.multiple_of(t * size, size), size)

    def recv_hot(t, carry):
        rows = place(t, TA)
        ids = receiver[pl.ds(t * (TA // 128), TA // 128)].reshape(TA // 128, 128)
        col = column(ids)
        recv_col[rows, :] = col.astype(I16)
        hot = pick(col & 511, 512)
        pick_recv[rows, :] = hot
        both = mm(hot, nodes2[...])
        stacked[rows, 2 * L :] = jnp.where(col >= 512, both[:, L:], both[:, :L]).astype(BF16)
        return carry

    loads[2].wait()
    loads[3].wait()
    lax.fori_loop(0, E // TA, recv_hot, 0)

    def send_hot(t, carry):
        rows = place(t, TA)
        ids = slot[pl.ds(t * (TA // 128), TA // 128)].reshape(TA // 128, 128)
        col = column(ids)
        send_col[rows, :] = col.astype(I16)
        pick_send[rows, :] = pick(col & 1023, 1024)
        return carry

    lax.fori_loop(0, E // TA, send_hot, 0)
    pl.semaphore_wait(barrier, len(greeted))
    for k in FAR_FIRST:
        ask(k).start()
    asked[me] = wanted[me]

    for copy in loads[4:]:
        copy.wait()

    def part_pre(t, carry):
        rows = place(t, T)
        both = jnp.concatenate([stacked[rows, :L], stacked[rows, 2 * L :]], axis=1)
        weight = jnp.concatenate([w_ein[:L, :], w_ein[2 * L :, :]], axis=0)
        big[rows, :] = mm(both, weight)
        return carry

    lax.fori_loop(0, E // T, part_pre, 0)

    def recv_spread(t, carry):
        ids = receiver[pl.ds(t * (TA // 128), TA // 128)].reshape(TA // 128, 128)
        spread_recv[t] = spread(ids & 511, 512)
        return carry

    lax.fori_loop(0, E // TA, recv_spread, 0)
    def look_up(ids):
        col = column(ids)
        both = mm(pick(col & 511, 512), nodes2[...])
        return jnp.where(col >= 512, both[:, L:], both[:, :L]).astype(BF16)

    rows_in[me] = look_up(asked[me])
    for batch in BATCHES:
        for k in batch:
            ask(k).wait_recv()
        found = look_up(jnp.concatenate([asked[behind(me, k)] for k in batch], axis=0))
        for i, k in enumerate(batch):
            staged[k] = found[128 * i : 128 * i + 128]
        for k in reversed(batch):
            give(k).start()


    for k in range(1, NB):
        ask(k).wait_send()
        give(k).wait()
    for p in range(8):
        slots2[128 * p : 128 * p + 128, :L] = rows_in[p]
        slots2[128 * p : 128 * p + 128, L:] = rows_in[p + 8]

    def cut(step):
        return slice(step * TA, step * TA + TA)

    def gather(rows):
        both = mm(pick_send[rows, :], slots2[...])
        high = send_col[rows, :].astype(jnp.int32) >= 1024
        stacked[rows, L : 2 * L] = jnp.where(high, both[:, L:], both[:, :L]).astype(BF16)

    def first(rows):
        pre = big[rows, :] + mm(stacked[rows, L : 2 * L], w_ein[L : 2 * L, :])
        hid, slp = silu_pair(pre)
        hidden[rows, :] = hid
        slope[rows, :] = slp.astype(BF16)

    def second(rows, t):
        norm, inv = layer_norm(mm(hidden[rows, :], w_eout[...]))
        big[rows, :L] = norm
        big[rows, L : 2 * L] = jnp.broadcast_to(inv, (TA, L))
        message = norm.astype(BF16).astype(F32)
        new_edges[rows, :] = (stacked[rows, :L].astype(F32) + message).astype(BF16)
        to_node = mm(spread_recv[t], halves(message, recv_col[rows, :].astype(jnp.int32) >= 512))
        acc_node[...] = to_node if t == 0 else acc_node[...] + to_node

    count = E // TA
    for step in range(count + 2):
        if step < count:
            gather(cut(step))
        if 1 <= step <= count:
            first(cut(step - 1))
        if step >= 2:
            second(cut(step - 2), step - 2)
    stores = [pltpu.make_async_copy(new_edges, new_edges_h, store_sem.at[0])]
    stores[0].start()

    inbound = jnp.concatenate([acc_node[:, :L], acc_node[:, L:]], axis=0).astype(BF16)
    node = nodes[...]
    node_input = jnp.concatenate([node, inbound], axis=1)
    hid, slp = silu_pair(mm(node_input, w_nin[...]))
    norm, inv = layer_norm(mm(hid, w_nout[...]))
    new_nodes[...] = (node.astype(F32) + norm).astype(BF16)
    stores.append(pltpu.make_async_copy(new_nodes, new_nodes_h, store_sem.at[1]))
    stores[1].start()
    cot = node_cot[...].astype(F32)
    d_out = norm_back(cot, norm, inv).astype(BF16)
    d_pre = (mm_nt(d_out, w_nout[...]) * slp).astype(BF16)
    d_in = mm_nt(d_pre, w_nin[...])
    d_inbound = d_in[:, L:].astype(BF16)
    nodes2[:, :L] = d_inbound[: GR // 2, :]
    nodes2[:, L:] = d_inbound[GR // 2 :, :]

    def node_grads():
        node_part[...] = cot + d_in[:, :L]
        store_block(total_n, 2, mm_tn(d_out, hid))
        g_in = mm_tn(node_input, d_pre)
        store_block(total_n, 0, g_in[:128])
        store_block(total_n, 1, g_in[128:])


    def gather_back(rows):
        both = mm(pick_recv[rows, :], nodes2[...])
        big[rows, 3 * L :] = jnp.where(recv_col[rows, :].astype(jnp.int32) >= 512, both[:, L:], both[:, :L])

    def back_norm(rows):
        upstream = edge_cot[rows, :].astype(F32) + big[rows, 3 * L :]
        d_out = norm_back(upstream, big[rows, :L], big[rows, L : 2 * L]).astype(BF16)
        d_out_all[rows, :] = d_out
        slope[rows, :] = (mm_nt(d_out, w_eout[...]) * slope[rows, :].astype(F32)).astype(BF16)

    def weight_grads(rows, t):
        g_in = mm_tn(stacked[rows, :], slope[rows, :])
        g_out = mm_tn(d_out_all[rows, :], hidden[rows, :])
        if t > 0:
            g_in = g_in + jnp.concatenate([acc_slot[:384, :], acc_slot[384:768, :]], axis=1)
            g_out = g_out + jnp.concatenate([acc_slot[768:896, :], acc_slot[896:, :]], axis=1)
        if t < count - 1:
            acc_slot[:384, :] = g_in[:, : H // 2]
            acc_slot[384:768, :] = g_in[:, H // 2 :]
            acc_slot[768:896, :] = g_out[:, : H // 2]
            acc_slot[896:, :] = g_out[:, H // 2 :]
        else:
            for b in range(3):
                store_block(total_e, b, g_in[128 * b : 128 * b + 128])
            store_block(total_e, 3, g_out)

    for step in range(count + 2):
        if step == 2:
            red_n.to_line()
        if step < count:
            gather_back(cut(step))
        if step == 0:
            node_grads()
            red_n.start()
        if 1 <= step <= count:
            back_norm(cut(step - 1))
        if step >= 2:
            weight_grads(cut(step - 2), step - 2)
    red_e.start()
    red_e.to_line()

    def back_input(rows):
        d_in = mm_nt(slope[rows, :], w_ein[...])
        big[rows, 2 * L : 3 * L] = edge_cot[rows, :].astype(F32) + d_in[:, :L]
        pick_send[rows, : 2 * L] = halves(d_in[:, L : 2 * L], send_col[rows, :].astype(jnp.int32) >= 1024)
        pick_send[rows, 2 * L : 4 * L] = halves(d_in[:, 2 * L :], recv_col[rows, :].astype(jnp.int32) >= 512)

    def scatter(rows, t):
        send = slot[TA // 128 * t : TA // 128 * (t + 1)].reshape(TA // 128, 128)
        to_slot = mm(spread(send & 1023, 1024), pick_send[rows, : 2 * L])
        to_node = mm(spread_recv[t], pick_send[rows, 2 * L : 4 * L])
        acc_slot[...] = to_slot if t == 0 else acc_slot[...] + to_slot
        acc_node[...] = to_node if t == 0 else acc_node[...] + to_node

    for step in range(count + 1):
        if step < count:
            back_input(cut(step))
        if step >= 1:
            scatter(cut(step - 1), step - 1)
        if step == 2:
            red_n.to_z()
    for p in range(8):
        slot_grad[p] = acc_slot[128 * p : 128 * p + 128, :L].astype(BF16)
        slot_grad[p + 8] = acc_slot[128 * p : 128 * p + 128, L:].astype(BF16)
    for k in FAR_FIRST:
        give_slot(k).start()
    slot_in[me] = slot_grad[me]
    stores.append(
        pltpu.make_async_copy(big.at[:, pl.ds(2 * L, L)], edge_grad_h, store_sem.at[2])
    )
    stores[2].start()
    red_n.to_all()
    node_part[: GR // 2, :] += acc_node[:, :L]
    node_part[GR // 2 :, :] += acc_node[:, L:]
    red_e.to_z()
    red_e.to_all()
    for k in range(1, NB):
        give_slot(k).wait()

    def home(q, carry):
        ids = asked[pl.ds(4 * q, 4)].reshape(4, 128)
        values = slot_in[pl.ds(4 * q, 4)].reshape(4 * 128, L)
        node_part[...] += mm(spread(ids, GR), values)
        return carry

    lax.fori_loop(0, NB // 4, home, 0)
    stores.append(pltpu.make_async_copy(node_part, node_grad_h, store_sem.at[5]))
    stores[3].start()
    core = lax.rem(grp, 2)
    red_n.to_pair()
    stores.append(pltpu.make_async_copy(out_n.at[core], out_nh.at[core], store_sem.at[3]))
    stores[4].start()
    red_e.to_pair()
    stores.append(pltpu.make_async_copy(out_e.at[core], out_h.at[core], store_sem.at[4]))
    stores[5].start()
    red_n.end()
    red_e.end()
    for copy in stores:
        copy.wait()


def main(*args):
    sem = pltpu.SemaphoreType.DMA
    vm = pltpu.VMEM

    def reduce_buffers(blocks):
        rows = 16 * blocks
        return [vm((2, NB, rows, L), BF16)] * 2 + [
            vm((NB, rows, L), BF16),
            vm((NB, rows, L), BF16),
            vm((NB, rows, L), BF16),
            vm((rows, L), BF16),
            vm((4, rows, L), BF16),
        ]

    return pl.pallas_call(
        main_kernel,
        name="message_passing",
        out_shape=(
            jax.ShapeDtypeStruct((GR, L), BF16),
            jax.ShapeDtypeStruct((E, L), BF16),
            jax.ShapeDtypeStruct((E, L), F32),
            jax.ShapeDtypeStruct((GR, L), F32),
            jax.ShapeDtypeStruct((2, NB, 16 * NODE, L), BF16),
            jax.ShapeDtypeStruct((2, NB, 16 * EDGE, L), BF16),
        ),
        in_specs=anywhere(11),
        out_specs=anywhere(6),
        scratch_shapes=[
            vm((NB, 1, 128), jnp.int32),
            vm((E // 128, 1, 128), jnp.int32),
            vm((E // 128, 1, 128), jnp.int32),
            vm((GR, L), BF16),
            vm((3 * L, H), BF16),
            vm((H, L), BF16),
            vm((2 * L, H), BF16),
            vm((H, L), BF16),
            vm((GR, L), BF16),
            vm((E, L), BF16),
            vm((NB, 1, 128), jnp.int32),
            vm((NB, 128, L), BF16),
            vm((NB, 128, L), BF16),
            vm((E, L), I16),
            vm((E, L), I16),
            vm((E, 512), BF16),
            vm((E, 1024), BF16),
            vm((E // TA, 512, TA), BF16),
            vm((E, 3 * L), BF16),
            vm((E, H), F32),
            vm((E, H), BF16),
            vm((E, H), BF16),
            vm((E, L), BF16),
            vm((GR, 2 * L), BF16),
            vm((GR // 2, 2 * L), BF16),
            vm((GR // 2, 2 * L), F32),
            vm((GR, 2 * L), F32),
            vm((GR, L), F32),
            vm((GR, L), BF16),
            vm((E, L), BF16),
            vm((NB, 128, L), BF16),
            vm((NB, 128, L), BF16),
        ]
        + reduce_buffers(NODE)
        + reduce_buffers(EDGE)
        + [sem((11,)), sem((6,))]
        + [sem((NB,))] * 6
        + [sem((5,)), sem((5,)), sem((2, NB)), sem((2, NB))] * 2,
        compiler_params=pltpu.CompilerParams(
            collective_id=0, has_side_effects=True, vmem_limit_bytes=VMEM_LIMIT
        ),
    )(*args)


def finish_kernel(edge_scale, node_scale, *refs):
    sources, targets, results = refs[:6], refs[6:10], refs[10:14]
    held, grads = refs[14:20], refs[20:24]
    load_sem, store_sem = refs[24:]
    loads = [pltpu.make_async_copy(sources[i], held[i], load_sem.at[i]) for i in range(6)]
    stores = [pltpu.make_async_copy(held[i + 2], targets[i], store_sem.at[i]) for i in range(4)]
    moves = [pltpu.make_async_copy(grads[i], results[i], store_sem.at[4 + i]) for i in range(4)]
    for copy in loads:
        copy.start()
    out_e, out_n = held[:2]
    g_ein, g_eout, g_nin, g_nout = grads
    loads[0].wait()
    for b in range(3):
        g_ein[128 * b : 128 * b + 128, :] = load_block(out_e, b, edge_scale)
    moves[0].start()
    g_eout[...] = jnp.transpose(load_block(out_e, 3, edge_scale))
    moves[1].start()
    loads[1].wait()
    for b in range(2):
        g_nin[128 * b : 128 * b + 128, :] = load_block(out_n, b, node_scale)
    moves[2].start()
    g_nout[...] = jnp.transpose(load_block(out_n, 2, node_scale))
    moves[3].start()
    for load, store in zip(loads[2:], stores):
        load.wait()
        store.start()
    for copy in moves + stores:
        copy.wait()


def finish(out_e, out_n, *arrays):
    grads = tuple(
        jax.ShapeDtypeStruct(shape, F32) for shape in ((3 * L, H), (H, L), (2 * L, H), (H, L))
    )
    return pl.pallas_call(
        functools.partial(
            finish_kernel, float((E * NB * NG) ** -0.5), float((GR * NB * NG) ** -0.5)
        ),
        name="finish",
        out_shape=tuple(jax.ShapeDtypeStruct(a.shape, a.dtype) for a in arrays) + grads,
        in_specs=anywhere(6),
        out_specs=anywhere(8),
        scratch_shapes=[pltpu.VMEM(a.shape, a.dtype) for a in (out_e, out_n) + arrays + grads]
        + [pltpu.SemaphoreType.DMA((6,)), pltpu.SemaphoreType.DMA((8,))],
        compiler_params=pltpu.CompilerParams(vmem_limit_bytes=VMEM_LIMIT),
    )(out_e, out_n, *arrays)


def on_device(
    nodes,
    edges,
    wanted_rows,
    sender_slot,
    receiver,
    w_edge_in,
    w_edge_out,
    w_node_in,
    w_node_out,
    node_cot,
    edge_cot,
):
    *arrays, out_n, out_e = main(
        wanted_rows.reshape(NB, 1, 128),
        sender_slot.reshape(E // 128, 1, 128),
        receiver.reshape(E // 128, 1, 128),
        nodes,
        edges,
        w_edge_in,
        w_edge_out,
        w_node_in,
        w_node_out,
        node_cot,
        edge_cot,
    )
    new_nodes, new_edges, edge_grad, node_grad, g_ein, g_eout, g_nin, g_nout = finish(
        out_e, out_n, *arrays
    )
    return new_nodes, new_edges, node_grad, edge_grad, g_ein, g_eout, g_nin, g_nout


def solution(mesh):
    split = P(("blk", "grp"), None)
    line = P(("blk", "grp"))
    return jax.shard_map(
        on_device,
        mesh=mesh,
        in_specs=(split, split, split, line, line, P(), P(), P(), P(), split, split),
        out_specs=(split, split, split, split, P(), P(), P(), P()),
        check_vma=False,
    )
```

```python
import functools

import jax
import jax.numpy as jnp
from jax import lax
from jax.experimental import pallas as pl
from jax.experimental.pallas import tpu as pltpu
from jax.sharding import PartitionSpec as P

EPSILON = 1e-05
L = 128
H = 512
NB = 16
NG = 8
GR = 1024
E = 4096
T = 2048
TA = 1024
TB = 1024
EDGE = 4
NODE = 3
F32 = jnp.float32
BF16 = jnp.bfloat16
I16 = jnp.int16
VMEM_LIMIT = 63 * 1024 * 1024
MESH = pl.DeviceIdType.MESH


def mm(a, b):
    return jnp.dot(a, b, preferred_element_type=F32)


def mm_nt(a, b):
    return lax.dot_general(a, b, (((1,), (1,)), ((), ())), preferred_element_type=F32)


def mm_tn(a, b):
    return lax.dot_general(a, b, (((0,), (0,)), ((), ())), preferred_element_type=F32)


def column(rows):
    parts = [
        jnp.transpose(jnp.broadcast_to(rows[i : i + 1, :], (128, 128)))
        for i in range(rows.shape[0])
    ]
    return parts[0] if len(parts) == 1 else jnp.concatenate(parts, axis=0)


def pick(col, width):
    col = col.astype(I16)
    lane = lax.broadcasted_iota(jnp.int32, col.shape, 1).astype(I16)
    one = jnp.ones(col.shape, BF16)
    zero = jnp.zeros(col.shape, BF16)
    return jnp.concatenate(
        [jnp.where(col == lane + I16(128 * j), one, zero) for j in range(width // 128)], axis=1
    )


def spread(rows, width):
    outs = []
    for i in range(rows.shape[0]):
        ids = jnp.broadcast_to(rows[i : i + 1, :], (128, 128)).astype(I16)
        sub = lax.broadcasted_iota(jnp.int32, (128, 128), 0).astype(I16)
        one = jnp.ones((128, 128), BF16)
        zero = jnp.zeros((128, 128), BF16)
        outs.append(
            jnp.concatenate(
                [jnp.where(ids == sub + I16(128 * j), one, zero) for j in range(width // 128)],
                axis=0,
            )
        )
    return outs[0] if len(outs) == 1 else jnp.concatenate(outs, axis=1)


def halves(value, high):
    zero = jnp.zeros_like(value)
    return jnp.concatenate(
        [jnp.where(high, zero, value), jnp.where(high, value, zero)], axis=1
    ).astype(BF16)


def layer_norm(value):
    center = value - jnp.mean(value, axis=-1, keepdims=True)
    inv = lax.rsqrt(jnp.mean(center * center, axis=-1, keepdims=True) + EPSILON)
    return center * inv, inv


def norm_back(upstream, normed, inv):
    first = jnp.mean(upstream, axis=-1, keepdims=True)
    second = jnp.mean(upstream * normed, axis=-1, keepdims=True)
    return (upstream - first - normed * second) * inv


def silu_pair(pre):
    sig = 0.5 * jnp.tanh(0.5 * pre) + 0.5
    hid = pre * sig
    return hid.astype(BF16), sig + hid * (1.0 - sig)


def whole(n):
    return [pl.BlockSpec(memory_space=pltpu.VMEM)] * n


def anywhere(n):
    return [pl.BlockSpec(memory_space=pl.ANY)] * n


def store_block(total, block, value):
    value = value.astype(BF16)
    for half in range(2):
        for i in range(4):
            for j in range(4):
                total[half, 4 * i + j, 16 * block : 16 * block + 16, :] = value[
                    64 * half + 16 * i : 64 * half + 16 * i + 16, 128 * j : 128 * j + 128
                ]


def load_block(out, block, scale):
    lines = []
    for half in range(2):
        for i in range(4):
            lines.append(
                jnp.concatenate(
                    [out[half, 4 * i + j, 16 * block : 16 * block + 16, :] for j in range(4)],
                    axis=1,
                )
            )
    return jnp.concatenate(lines, axis=0).astype(F32) * scale


def distance(k):
    dx, dy = k // 4, k % 4
    return min(dx, 4 - dx) + min(dy, 4 - dy)


FAR_FIRST = sorted(range(1, NB), key=distance, reverse=True)
BATCHES = [[k for k in range(1, NB) if distance(k) in near] for near in ((1,), (2,), (3, 4))]


def ahead(me, k):
    return lax.rem(me // 4 + k // 4, 4) * 4 + lax.rem(lax.rem(me, 4) + k % 4, 4)


def behind(me, k):
    return lax.rem(me // 4 + 4 - k // 4, 4) * 4 + lax.rem(lax.rem(me, 4) + 4 - k % 4, 4)


def remote(src, dst, send, recv, to):
    return pltpu.make_async_remote_copy(
        src_ref=src, dst_ref=dst, send_sem=send, recv_sem=recv, device_id=to, device_id_type=MESH
    )


class Reduce:
    def __init__(self, me, grp, total, out, target, half_in, mine, piece_in, own, z_in, sems):
        self.me, self.grp = me, grp
        self.core = lax.rem(grp, 2)
        self.zpos = grp // 2
        self.other = (me, grp + 1 - 2 * self.core)
        self.total, self.out, self.target = total, out, target
        self.half_in, self.mine = half_in, mine
        self.piece_in, self.own, self.z_in = piece_in, own, z_in
        self.ps, self.pr, self.ls, self.lr = sems

    def pair(self):
        return remote(
            self.total.at[1 - self.core], self.half_in, self.ps.at[0], self.pr.at[0], self.other
        )

    def piece(self, k):
        to = ahead(self.me, k)
        return remote(
            self.mine.at[to],
            self.piece_in.at[self.me],
            self.ls.at[0, k],
            self.lr.at[0, k],
            (to, self.grp),
        )

    def along_z(self, k):
        to = lax.rem(self.grp + 2 * k, NG)
        return remote(
            self.own, self.z_in.at[self.zpos], self.ps.at[1 + k], self.pr.at[1 + k], (self.me, to)
        )

    def spread(self, k):
        to = ahead(self.me, k)
        place = self.out.at[self.core, self.me]
        return remote(place, place, self.ls.at[1, k], self.lr.at[1, k], (to, self.grp))

    def last(self):
        return remote(
            self.out.at[self.core],
            self.target.at[self.core],
            self.ps.at[1],
            self.pr.at[1],
            self.other,
        )

    def start(self):
        self.pair().start()

    def to_line(self):
        self.pair().wait()
        self.mine[...] = (
            self.total[self.core].astype(F32) + self.half_in[...].astype(F32)
        ).astype(BF16)
        for k in FAR_FIRST:
            self.piece(k).start()
        self.piece_in[self.me] = self.mine[self.me]

    def to_z(self):
        for k in range(1, NB):
            self.piece(k).wait()
        acc = self.piece_in[0].astype(F32)
        for q in range(1, NB):
            acc = acc + self.piece_in[q].astype(F32)
        self.own[...] = acc.astype(BF16)
        for k in range(1, 4):
            self.along_z(k).start()
        self.z_in[self.zpos] = self.own[...]

    def to_all(self):
        for k in range(1, 4):
            self.along_z(k).wait()
        acc = self.z_in[0].astype(F32)
        for q in range(1, 4):
            acc = acc + self.z_in[q].astype(F32)
        self.out[self.core, self.me] = acc.astype(BF16)
        for k in FAR_FIRST:
            self.spread(k).start()

    def to_pair(self):
        for k in range(1, NB):
            self.spread(k).wait()
        self.last().start()

    def end(self):
        self.last().wait()


def main_kernel(
    wanted_h,
    slot_h,
    receiver_h,
    nodes_h,
    edges_h,
    w_ein_h,
    w_eout_h,
    w_nin_h,
    w_nout_h,
    node_cot_h,
    edge_cot_h,
    new_nodes_h,
    new_edges_h,
    edge_grad_h,
    node_grad_h,
    out_nh,
    out_h,
    wanted,
    slot,
    receiver,
    nodes,
    w_ein,
    w_eout,
    w_nin,
    w_nout,
    node_cot,
    edge_cot,
    asked,
    staged,
    rows_in,
    recv_col,
    send_col,
    pick_recv,
    pick_send,
    spread_recv,
    stacked,
    big,
    hidden,
    slope,
    d_out_all,
    slots2,
    nodes2,
    acc_node,
    acc_slot,
    node_part,
    new_nodes,
    new_edges,
    slot_grad,
    slot_in,
    total_n,
    out_n,
    half_n,
    mine_n,
    piece_n,
    own_n,
    z_n,
    total_e,
    out_e,
    half_e,
    mine_e,
    piece_e,
    own_e,
    z_e,
    load_sem,
    store_sem,
    s1,
    r1,
    s2,
    r2,
    s3,
    r3,
    n_ps,
    n_pr,
    n_ls,
    n_lr,
    e_ps,
    e_pr,
    e_ls,
    e_lr,
):
    me = lax.axis_index("blk")
    grp = lax.axis_index("grp")
    barrier = pltpu.get_barrier_semaphore()
    greeted = [(ahead(me, k), grp) for k in FAR_FIRST]
    greeted += [(me, lax.rem(grp + 2 * k, NG)) for k in range(1, 4)]
    greeted += [(me, grp + 1 - 2 * lax.rem(grp, 2))]
    for peer in greeted:
        pl.semaphore_signal(barrier, inc=1, device_id=peer, device_id_type=MESH)

    loads = [
        pltpu.make_async_copy(src, dst, load_sem.at[i])
        for i, (src, dst) in enumerate(
            [
                (nodes_h, nodes),
                (receiver_h, receiver),
                (wanted_h, wanted),
                (slot_h, slot),
                (edges_h, stacked.at[:, pl.ds(0, L)]),
                (w_ein_h, w_ein),
                (w_eout_h, w_eout),
                (w_nin_h, w_nin),
                (w_nout_h, w_nout),
                (node_cot_h, node_cot),
                (edge_cot_h, edge_cot),
            ]
        )
    ]
    for copy in loads:
        copy.start()

    red_n = Reduce(
        me,
        grp,
        total_n,
        out_n,
        out_nh,
        half_n,
        mine_n,
        piece_n,
        own_n,
        z_n,
        (n_ps, n_pr, n_ls, n_lr),
    )
    red_e = Reduce(
        me,
        grp,
        total_e,
        out_e,
        out_h,
        half_e,
        mine_e,
        piece_e,
        own_e,
        z_e,
        (e_ps, e_pr, e_ls, e_lr),
    )

    def ask(k):
        to = ahead(me, k)
        return remote(wanted.at[to], asked.at[me], s1.at[k], r1.at[k], (to, grp))

    def give(k):
        to = behind(me, k)
        return remote(staged.at[k], rows_in.at[me], s2.at[k], r2.at[k], (to, grp))

    def give_slot(k):
        to = ahead(me, k)
        return remote(slot_grad.at[to], slot_in.at[me], s3.at[k], r3.at[k], (to, grp))

    loads[0].wait()
    loads[1].wait()
    nodes2[:, :L] = nodes[: GR // 2, :]
    nodes2[:, L:] = nodes[GR // 2 :, :]

    def place(t, size):
        return pl.ds(pl.multiple_of(t * size, size), size)

    def recv_hot(t, carry):
        rows = place(t, TA)
        ids = receiver[pl.ds(t * (TA // 128), TA // 128)].reshape(TA // 128, 128)
        col = column(ids)
        recv_col[rows, :] = col.astype(I16)
        hot = pick(col & 511, 512)
        pick_recv[rows, :] = hot
        both = mm(hot, nodes2[...])
        stacked[rows, 2 * L :] = jnp.where(col >= 512, both[:, L:], both[:, :L]).astype(BF16)
        return carry

    loads[2].wait()
    loads[3].wait()
    lax.fori_loop(0, E // TA, recv_hot, 0)

    def send_hot(t, carry):
        rows = place(t, TA)
        ids = slot[pl.ds(t * (TA // 128), TA // 128)].reshape(TA // 128, 128)
        col = column(ids)
        send_col[rows, :] = col.astype(I16)
        pick_send[rows, :] = pick(col & 1023, 1024)
        return carry

    lax.fori_loop(0, E // TA, send_hot, 0)
    pl.semaphore_wait(barrier, len(greeted))
    for k in FAR_FIRST:
        ask(k).start()
    asked[me] = wanted[me]

    for copy in loads[4:]:
        copy.wait()

    def part_pre(t, carry):
        rows = place(t, T)
        both = jnp.concatenate([stacked[rows, :L], stacked[rows, 2 * L :]], axis=1)
        weight = jnp.concatenate([w_ein[:L, :], w_ein[2 * L :, :]], axis=0)
        big[rows, :] = mm(both, weight)
        return carry

    lax.fori_loop(0, E // T, part_pre, 0)

    def recv_spread(t, carry):
        ids = receiver[pl.ds(t * (TA // 128), TA // 128)].reshape(TA // 128, 128)
        spread_recv[t] = spread(ids & 511, 512)
        return carry

    lax.fori_loop(0, E // TA, recv_spread, 0)
    def look_up(ids):
        col = column(ids)
        both = mm(pick(col & 511, 512), nodes2[...])
        return jnp.where(col >= 512, both[:, L:], both[:, :L]).astype(BF16)

    rows_in[me] = look_up(asked[me])
    for batch in BATCHES:
        for k in batch:
            ask(k).wait_recv()
        found = look_up(jnp.concatenate([asked[behind(me, k)] for k in batch], axis=0))
        for i, k in enumerate(batch):
            staged[k] = found[128 * i : 128 * i + 128]
        for k in reversed(batch):
            give(k).start()


    for k in range(1, NB):
        ask(k).wait_send()
        give(k).wait()
    for p in range(8):
        slots2[128 * p : 128 * p + 128, :L] = rows_in[p]
        slots2[128 * p : 128 * p + 128, L:] = rows_in[p + 8]

    def cut(step):
        return slice(step * TA, step * TA + TA)

    def gather(rows):
        both = mm(pick_send[rows, :], slots2[...])
        high = send_col[rows, :].astype(jnp.int32) >= 1024
        stacked[rows, L : 2 * L] = jnp.where(high, both[:, L:], both[:, :L]).astype(BF16)

    def first(rows):
        pre = big[rows, :] + mm(stacked[rows, L : 2 * L], w_ein[L : 2 * L, :])
        hid, slp = silu_pair(pre)
        hidden[rows, :] = hid
        slope[rows, :] = slp.astype(BF16)

    def second(rows, t):
        norm, inv = layer_norm(mm(hidden[rows, :], w_eout[...]))
        big[rows, :L] = norm
        big[rows, L : 2 * L] = jnp.broadcast_to(inv, (TA, L))
        message = norm.astype(BF16).astype(F32)
        new_edges[rows, :] = (stacked[rows, :L].astype(F32) + message).astype(BF16)
        to_node = mm(spread_recv[t], halves(message, recv_col[rows, :].astype(jnp.int32) >= 512))
        acc_node[...] = to_node if t == 0 else acc_node[...] + to_node

    count = E // TA
    for step in range(count + 2):
        if step < count:
            gather(cut(step))
        if 1 <= step <= count:
            first(cut(step - 1))
        if step >= 2:
            second(cut(step - 2), step - 2)
    stores = [pltpu.make_async_copy(new_edges, new_edges_h, store_sem.at[0])]
    stores[0].start()

    inbound = jnp.concatenate([acc_node[:, :L], acc_node[:, L:]], axis=0).astype(BF16)
    node = nodes[...]
    node_input = jnp.concatenate([node, inbound], axis=1)
    hid, slp = silu_pair(mm(node_input, w_nin[...]))
    norm, inv = layer_norm(mm(hid, w_nout[...]))
    new_nodes[...] = (node.astype(F32) + norm).astype(BF16)
    stores.append(pltpu.make_async_copy(new_nodes, new_nodes_h, store_sem.at[1]))
    stores[1].start()
    cot = node_cot[...].astype(F32)
    d_out = norm_back(cot, norm, inv).astype(BF16)
    d_pre = (mm_nt(d_out, w_nout[...]) * slp).astype(BF16)
    d_in = mm_nt(d_pre, w_nin[...])
    d_inbound = d_in[:, L:].astype(BF16)
    nodes2[:, :L] = d_inbound[: GR // 2, :]
    nodes2[:, L:] = d_inbound[GR // 2 :, :]

    def node_grads():
        node_part[...] = cot + d_in[:, :L]
        store_block(total_n, 2, mm_tn(d_out, hid))
        g_in = mm_tn(node_input, d_pre)
        store_block(total_n, 0, g_in[:128])
        store_block(total_n, 1, g_in[128:])


    def gather_back(rows):
        both = mm(pick_recv[rows, :], nodes2[...])
        big[rows, 3 * L :] = jnp.where(recv_col[rows, :].astype(jnp.int32) >= 512, both[:, L:], both[:, :L])

    def back_norm(rows):
        upstream = edge_cot[rows, :].astype(F32) + big[rows, 3 * L :]
        d_out = norm_back(upstream, big[rows, :L], big[rows, L : 2 * L]).astype(BF16)
        d_out_all[rows, :] = d_out
        slope[rows, :] = (mm_nt(d_out, w_eout[...]) * slope[rows, :].astype(F32)).astype(BF16)

    def weight_grads(rows, t):
        g_in = mm_tn(stacked[rows, :], slope[rows, :])
        g_out = mm_tn(d_out_all[rows, :], hidden[rows, :])
        if t > 0:
            g_in = g_in + jnp.concatenate([acc_slot[:384, :], acc_slot[384:768, :]], axis=1)
            g_out = g_out + jnp.concatenate([acc_slot[768:896, :], acc_slot[896:, :]], axis=1)
        if t < count - 1:
            acc_slot[:384, :] = g_in[:, : H // 2]
            acc_slot[384:768, :] = g_in[:, H // 2 :]
            acc_slot[768:896, :] = g_out[:, : H // 2]
            acc_slot[896:, :] = g_out[:, H // 2 :]
        else:
            for b in range(3):
                store_block(total_e, b, g_in[128 * b : 128 * b + 128])
            store_block(total_e, 3, g_out)

    for step in range(count + 2):
        if step == 2:
            red_n.to_line()
        if step < count:
            gather_back(cut(step))
        if step == 0:
            node_grads()
            red_n.start()
        if 1 <= step <= count:
            back_norm(cut(step - 1))
        if step >= 2:
            weight_grads(cut(step - 2), step - 2)
    red_e.start()

    def back_input(rows):
        d_in = mm_nt(slope[rows, :], w_ein[...])
        big[rows, 2 * L : 3 * L] = edge_cot[rows, :].astype(F32) + d_in[:, :L]
        pick_send[rows, : 2 * L] = halves(d_in[:, L : 2 * L], send_col[rows, :].astype(jnp.int32) >= 1024)
        pick_send[rows, 2 * L : 4 * L] = halves(d_in[:, 2 * L :], recv_col[rows, :].astype(jnp.int32) >= 512)

    def scatter(rows, t):
        send = slot[TA // 128 * t : TA // 128 * (t + 1)].reshape(TA // 128, 128)
        to_slot = mm(spread(send & 1023, 1024), pick_send[rows, : 2 * L])
        to_node = mm(spread_recv[t], pick_send[rows, 2 * L : 4 * L])
        acc_slot[...] = to_slot if t == 0 else acc_slot[...] + to_slot
        acc_node[...] = to_node if t == 0 else acc_node[...] + to_node

    for step in range(count + 1):
        if step < count:
            back_input(cut(step))
        if step == 0:
            red_e.to_line()
        if step == count:
            red_e.to_z()
        if step >= 1:
            scatter(cut(step - 1), step - 1)
        if step == 2:
            red_n.to_z()
    for p in range(8):
        slot_grad[p] = acc_slot[128 * p : 128 * p + 128, :L].astype(BF16)
        slot_grad[p + 8] = acc_slot[128 * p : 128 * p + 128, L:].astype(BF16)
    for k in FAR_FIRST:
        give_slot(k).start()
    slot_in[me] = slot_grad[me]
    stores.append(
        pltpu.make_async_copy(big.at[:, pl.ds(2 * L, L)], edge_grad_h, store_sem.at[2])
    )
    stores[2].start()
    red_n.to_all()
    node_part[: GR // 2, :] += acc_node[:, :L]
    node_part[GR // 2 :, :] += acc_node[:, L:]
    red_e.to_all()
    for k in range(1, NB):
        give_slot(k).wait()

    def home(q, carry):
        ids = asked[pl.ds(4 * q, 4)].reshape(4, 128)
        values = slot_in[pl.ds(4 * q, 4)].reshape(4 * 128, L)
        node_part[...] += mm(spread(ids, GR), values)
        return carry

    lax.fori_loop(0, NB // 4, home, 0)
    stores.append(pltpu.make_async_copy(node_part, node_grad_h, store_sem.at[5]))
    stores[3].start()
    core = lax.rem(grp, 2)
    red_n.to_pair()
    stores.append(pltpu.make_async_copy(out_n.at[core], out_nh.at[core], store_sem.at[3]))
    stores[4].start()
    red_e.to_pair()
    stores.append(pltpu.make_async_copy(out_e.at[core], out_h.at[core], store_sem.at[4]))
    stores[5].start()
    red_n.end()
    red_e.end()
    for copy in stores:
        copy.wait()


def main(*args):
    sem = pltpu.SemaphoreType.DMA
    vm = pltpu.VMEM

    def reduce_buffers(blocks):
        rows = 16 * blocks
        return [vm((2, NB, rows, L), BF16)] * 2 + [
            vm((NB, rows, L), BF16),
            vm((NB, rows, L), BF16),
            vm((NB, rows, L), BF16),
            vm((rows, L), BF16),
            vm((4, rows, L), BF16),
        ]

    return pl.pallas_call(
        main_kernel,
        name="message_passing",
        out_shape=(
            jax.ShapeDtypeStruct((GR, L), BF16),
            jax.ShapeDtypeStruct((E, L), BF16),
            jax.ShapeDtypeStruct((E, L), F32),
            jax.ShapeDtypeStruct((GR, L), F32),
            jax.ShapeDtypeStruct((2, NB, 16 * NODE, L), BF16),
            jax.ShapeDtypeStruct((2, NB, 16 * EDGE, L), BF16),
        ),
        in_specs=anywhere(11),
        out_specs=anywhere(6),
        scratch_shapes=[
            vm((NB, 1, 128), jnp.int32),
            vm((E // 128, 1, 128), jnp.int32),
            vm((E // 128, 1, 128), jnp.int32),
            vm((GR, L), BF16),
            vm((3 * L, H), BF16),
            vm((H, L), BF16),
            vm((2 * L, H), BF16),
            vm((H, L), BF16),
            vm((GR, L), BF16),
            vm((E, L), BF16),
            vm((NB, 1, 128), jnp.int32),
            vm((NB, 128, L), BF16),
            vm((NB, 128, L), BF16),
            vm((E, L), I16),
            vm((E, L), I16),
            vm((E, 512), BF16),
            vm((E, 1024), BF16),
            vm((E // TA, 512, TA), BF16),
            vm((E, 3 * L), BF16),
            vm((E, H), F32),
            vm((E, H), BF16),
            vm((E, H), BF16),
            vm((E, L), BF16),
            vm((GR, 2 * L), BF16),
            vm((GR // 2, 2 * L), BF16),
            vm((GR // 2, 2 * L), F32),
            vm((GR, 2 * L), F32),
            vm((GR, L), F32),
            vm((GR, L), BF16),
            vm((E, L), BF16),
            vm((NB, 128, L), BF16),
            vm((NB, 128, L), BF16),
        ]
        + reduce_buffers(NODE)
        + reduce_buffers(EDGE)
        + [sem((11,)), sem((6,))]
        + [sem((NB,))] * 6
        + [sem((5,)), sem((5,)), sem((2, NB)), sem((2, NB))] * 2,
        compiler_params=pltpu.CompilerParams(
            collective_id=0, has_side_effects=True, vmem_limit_bytes=VMEM_LIMIT
        ),
    )(*args)


def finish_kernel(edge_scale, node_scale, *refs):
    sources, targets, results = refs[:6], refs[6:10], refs[10:14]
    held, grads = refs[14:20], refs[20:24]
    load_sem, store_sem = refs[24:]
    loads = [pltpu.make_async_copy(sources[i], held[i], load_sem.at[i]) for i in range(6)]
    stores = [pltpu.make_async_copy(held[i + 2], targets[i], store_sem.at[i]) for i in range(4)]
    moves = [pltpu.make_async_copy(grads[i], results[i], store_sem.at[4 + i]) for i in range(4)]
    for copy in loads:
        copy.start()
    out_e, out_n = held[:2]
    g_ein, g_eout, g_nin, g_nout = grads
    loads[0].wait()
    for b in range(3):
        g_ein[128 * b : 128 * b + 128, :] = load_block(out_e, b, edge_scale)
    moves[0].start()
    g_eout[...] = jnp.transpose(load_block(out_e, 3, edge_scale))
    moves[1].start()
    loads[1].wait()
    for b in range(2):
        g_nin[128 * b : 128 * b + 128, :] = load_block(out_n, b, node_scale)
    moves[2].start()
    g_nout[...] = jnp.transpose(load_block(out_n, 2, node_scale))
    moves[3].start()
    for load, store in zip(loads[2:], stores):
        load.wait()
        store.start()
    for copy in moves + stores:
        copy.wait()


def finish(out_e, out_n, *arrays):
    grads = tuple(
        jax.ShapeDtypeStruct(shape, F32) for shape in ((3 * L, H), (H, L), (2 * L, H), (H, L))
    )
    return pl.pallas_call(
        functools.partial(
            finish_kernel, float((E * NB * NG) ** -0.5), float((GR * NB * NG) ** -0.5)
        ),
        name="finish",
        out_shape=tuple(jax.ShapeDtypeStruct(a.shape, a.dtype) for a in arrays) + grads,
        in_specs=anywhere(6),
        out_specs=anywhere(8),
        scratch_shapes=[pltpu.VMEM(a.shape, a.dtype) for a in (out_e, out_n) + arrays + grads]
        + [pltpu.SemaphoreType.DMA((6,)), pltpu.SemaphoreType.DMA((8,))],
        compiler_params=pltpu.CompilerParams(vmem_limit_bytes=VMEM_LIMIT),
    )(out_e, out_n, *arrays)


def on_device(
    nodes,
    edges,
    wanted_rows,
    sender_slot,
    receiver,
    w_edge_in,
    w_edge_out,
    w_node_in,
    w_node_out,
    node_cot,
    edge_cot,
):
    *arrays, out_n, out_e = main(
        wanted_rows.reshape(NB, 1, 128),
        sender_slot.reshape(E // 128, 1, 128),
        receiver.reshape(E // 128, 1, 128),
        nodes,
        edges,
        w_edge_in,
        w_edge_out,
        w_node_in,
        w_node_out,
        node_cot,
        edge_cot,
    )
    new_nodes, new_edges, edge_grad, node_grad, g_ein, g_eout, g_nin, g_nout = finish(
        out_e, out_n, *arrays
    )
    return new_nodes, new_edges, node_grad, edge_grad, g_ein, g_eout, g_nin, g_nout


def solution(mesh):
    split = P(("blk", "grp"), None)
    line = P(("blk", "grp"))
    return jax.shard_map(
        on_device,
        mesh=mesh,
        in_specs=(split, split, split, line, line, P(), P(), P(), P(), split, split),
        out_specs=(split, split, split, split, P(), P(), P(), P()),
        check_vma=False,
    )
```
